256 devices in a mesh: dp: 32 (over y, z), val: 8 (over x, core).
Axes of the slice: x: 4, y: 4, z: 8, core: 2. Of those that a mesh axis runs over, the one named last changes fastest.
Arguments:
- data: bfloat16 [256, 65536], P('dp', 'val'), may hold values from -24 to 24
- noise: bfloat16 [256, 65536], P('dp', 'val'), may hold values from -24 to 24
- times: float32 [256], P('dp'), may hold values from 0.05 to 0.95
- w_patch: bfloat16 [64, 1536], replicated, may hold values from -0.75 to 0.75
- patch_bias: float32 [1536], replicated, may hold values from -3 to 3
- norm_gain: float32 [1536], replicated, may hold values from 0.25 to 1.75
- w_qkv: bfloat16 [1536, 4608], P('dp'), may hold values from -0.15625 to 0.15625
Outputs:
- qkv: bfloat16 [256, 1024, 4608], P('dp', 'val')
- target: bfloat16 [256, 65536], P('dp', 'val')
The draws below stay inside these ranges and needn't reach their ends.
All inputs are finite; a program needn't handle non-finite values.
Results may differ from the reference program's by a relative error of at most 0.0057.
Values may be sent and summed in bfloat16 or wider, within the bound.
No kernel may reach another device: no remote copies, remote signals or barrier semaphores. Data moves between devices by JAX's collectives and lax.ppermute only.
A program may use at most 192 MiB of HBM per device.

```python
import jax
import jax.numpy as jnp
from jax import lax

HID = 1536
CH = 16
HH = 64
WW = 64
ITERS = 4
B = 256
V = 65536
TOK = 1024


def latent_rows(key):
    base = jnp.clip(jax.random.normal(key, (B, CH * HH * WW), jnp.float32), -6.0, 6.0)
    return base.astype(jnp.bfloat16)


def draw_data(key, part):
    key = jax.random.fold_in(key, 1)
    return latent_rows(key)


def draw_noise(key, part):
    key = jax.random.fold_in(key, 2)
    return latent_rows(key)


def shard_levels(own_key, shape, pieces, low, largest):
    loudness, own = 1.0, jax.random.fold_in(own_key, 6)
    for dim, shards_of in pieces:
        heights = jnp.exp(jax.random.uniform(jax.random.fold_in(own, dim), (shards_of,), jnp.float32, low / len(pieces), largest / len(pieces)))
        loudness = loudness * jnp.repeat(heights, shape[dim] // shards_of).reshape([-1 if axis == dim else 1 for axis in range(len(shape))])
    return loudness


def normal_values(stream_key, shape, scale, limit, split=(), kind=jnp.bfloat16):
    loudness = shard_levels(stream_key, shape, split, -0.22, 0.18) if split else 1.0
    drawn = jax.random.normal(stream_key, shape, jnp.float32) * scale * loudness
    return jnp.minimum(jnp.maximum(drawn, -limit), limit).astype(kind)


def setup_inputs(seed: int = 0) -> dict:
    key_list = jax.random.split(jax.random.key(seed), 8)
    data = draw_data(jax.random.fold_in(key_list[7], 71), 0)
    noise = draw_noise(jax.random.fold_in(key_list[7], 71), 0)
    times = jnp.clip(0.05 + 0.9 * jax.random.uniform(key_list[2], (B,), jnp.float32) ** shard_levels(key_list[2], (B,), ((0, 32),), -0.2, 0.2), 0.05, 0.95)
    w_patch = normal_values(key_list[3], (4 * CH, HID), (4 * CH) ** -0.5, 0.75)
    patch_bias = normal_values(key_list[4], (HID,), 0.5, 3.0, (), jnp.float32)
    norm_gain = jnp.clip(1.0 + 0.15 * jax.random.normal(key_list[5], (HID,), jnp.float32), 0.25, 1.75)
    w_qkv = normal_values(key_list[6], (HID, 3 * HID), HID ** -0.5, 0.15625, ((0, 32),))
    return dict(data=data, noise=noise, times=times, w_patch=w_patch, patch_bias=patch_bias, norm_gain=norm_gain, w_qkv=w_qkv)


blur = 0.1

def patches(latent):
    grid = latent.reshape(CH, HH // 2, 2, WW // 2, 2)
    grid = jnp.transpose(grid, (1, 3, 0, 2, 4))
    return grid.reshape(TOK, CH * 4)

def reference(data, noise, times, w_patch, patch_bias, norm_gain, w_qkv):
    cross = lax.dot_general(data, noise, (((1,), (1,)), ((), ())), preferred_element_type=jnp.float32)
    cost = -cross / jnp.sqrt(jnp.float32(V))
    col_pot = jnp.zeros((B,), jnp.float32)
    for step in range(ITERS):
        row_pot = -blur * jax.nn.logsumexp((col_pot[None, :] - cost) / blur, axis=1)
        col_pot = -blur * jax.nn.logsumexp((row_pot[:, None] - cost) / blur, axis=0)
    weights = jax.nn.softmax((col_pot[None, :] - cost) / blur, axis=1).astype(jnp.bfloat16)
    coupled = jnp.dot(weights, noise, preferred_element_type=jnp.float32)
    blend = times[:, None]
    mixed = ((1.0 - blend) * coupled + blend * data.astype(jnp.float32)).astype(jnp.bfloat16)
    target = (data.astype(jnp.float32) - coupled).astype(jnp.bfloat16)

    def one_row(latent):
        embed = jnp.dot(patches(latent), w_patch, preferred_element_type=jnp.float32) + patch_bias
        center = embed - lax.optimization_barrier(jnp.mean(embed, axis=1, keepdims=True))
        spread = lax.optimization_barrier(jnp.mean(center * center, axis=1, keepdims=True))
        normed = (center / jnp.sqrt(spread + 1e-05) * norm_gain).astype(jnp.bfloat16)
        return jnp.dot(normed, w_qkv, preferred_element_type=jnp.float32).astype(jnp.bfloat16)
    qkv = lax.map(one_row, mixed)
    return (qkv, target)
```

```python
import jax
import jax.numpy as jnp
from jax import lax
from jax.experimental import pallas as pl
from jax.experimental.pallas import tpu as pltpu
from jax.sharding import PartitionSpec as P

CH = 16
HH = 64
WW = 64
ITERS = 4


blur = 0.1


def sinkhorn_kernel(scale, cross_ref, noise_ref, coupled_ref):
    scores = cross_ref[...] * scale
    col = jnp.zeros((1, scores.shape[1]), jnp.float32)
    for step in range(ITERS):
        shifted = scores + col
        top = jnp.max(shifted, axis=1, keepdims=True)
        total = jnp.sum(jnp.exp(shifted - top), axis=1, keepdims=True)
        row = -(top + jnp.log(total))
        shifted = scores + row
        top = jnp.max(shifted, axis=0, keepdims=True)
        total = jnp.sum(jnp.exp(shifted - top), axis=0, keepdims=True)
        col = -(top + jnp.log(total))
    shifted = scores + col
    top = jnp.max(shifted, axis=1, keepdims=True)
    grown = jnp.exp(shifted - top)
    weights = (grown / jnp.sum(grown, axis=1, keepdims=True)).astype(jnp.bfloat16)
    coupled_ref[...] = jnp.dot(weights, noise_ref[...], preferred_element_type=jnp.float32)


def per_device(data, noise, times, w_patch, patch_bias, norm_gain, w_qkv):
    row_count, val_width = data.shape
    dp_devices = lax.axis_size("dp")
    val_devices = lax.axis_size("val")
    rows = row_count * dp_devices
    part = val_width // dp_devices
    everyone = ("dp", "val")
    local_chan = CH // val_devices
    half_wide = WW // 2
    local_tok = HH // 2 * half_wide // val_devices
    w_all = lax.all_gather(w_qkv, "dp", axis=0, tiled=True)
    pair = jnp.concatenate([data, noise], axis=0)
    pair = jnp.transpose(pair.reshape(2 * row_count, dp_devices, part), (1, 0, 2))
    pair = lax.all_to_all(pair, "dp", split_axis=0, concat_axis=0, tiled=True)
    data_part = pair[:, :row_count].reshape(rows, part)
    noise_part = pair[:, row_count:].reshape(rows, part)
    cross = lax.dot_general(
        data_part, noise_part, (((1,), (1,)), ((), ())), preferred_element_type=jnp.float32
    )
    cross = cross.reshape(rows, rows // 128, 128)
    cross = lax.all_to_all(cross, everyone, split_axis=0, concat_axis=0, tiled=True)
    own = jnp.sum(cross, axis=0, keepdims=True)
    own = jnp.broadcast_to(own, (rows, rows // 128, 128))
    cross = lax.all_to_all(own, everyone, split_axis=0, concat_axis=0, tiled=True)
    cross = cross.reshape(rows, rows)
    scale = 1.0 / (float(val_width * val_devices) ** 0.5 * blur)
    coupled = pl.pallas_call(
        lambda *refs: sinkhorn_kernel(scale, *refs),
        out_shape=jax.ShapeDtypeStruct((rows, part), jnp.float32),
        in_specs=[pl.BlockSpec(memory_space=pltpu.VMEM)] * 2,
        out_specs=pl.BlockSpec(memory_space=pltpu.VMEM),
        compiler_params=pltpu.CompilerParams(vmem_limit_bytes=16 * 2**20),
    )(cross, noise_part)
    coupled = coupled.reshape(dp_devices, row_count, part)
    coupled = lax.all_to_all(coupled, "dp", split_axis=0, concat_axis=0, tiled=True)
    coupled = jnp.transpose(coupled, (1, 0, 2)).reshape(row_count, val_width)
    blend = times[:, None]
    mixed = ((1.0 - blend) * coupled + blend * data.astype(jnp.float32)).astype(jnp.bfloat16)
    target = (data.astype(jnp.float32) - coupled).astype(jnp.bfloat16)
    grid = mixed.reshape(row_count, local_chan, HH, WW)
    blocks = grid.reshape(row_count, local_chan, val_devices, HH // val_devices * WW)
    moved = lax.all_to_all(blocks, "val", split_axis=2, concat_axis=1, tiled=True)
    moved = moved.reshape(row_count, CH, HH // val_devices // 2, 2, half_wide, 2)
    moved = jnp.transpose(moved, (0, 2, 4, 1, 3, 5)).reshape(row_count * local_tok, CH * 4)
    embed = jnp.dot(moved, w_patch, preferred_element_type=jnp.float32)
    embed = embed.reshape(row_count, local_tok, -1)
    embed = embed.reshape(row_count * local_tok, -1) + patch_bias
    center = embed - jnp.mean(embed, axis=1, keepdims=True)
    spread = jnp.mean(center * center, axis=1, keepdims=True)
    normed = (center / jnp.sqrt(spread + 1e-05) * norm_gain).astype(jnp.bfloat16)
    projected = jnp.dot(normed, w_all, preferred_element_type=jnp.float32)
    qkv = projected.reshape(row_count, local_tok, w_qkv.shape[1]).astype(jnp.bfloat16)
    return (qkv, target)


def solution(mesh):
    return jax.shard_map(
        per_device,
        mesh=mesh,
        in_specs=(P("dp", "val"), P("dp", "val"), P("dp"), P(), P(), P(), P("dp", None)),
        out_specs=(P("dp", "val", None), P("dp", "val")),
        check_vma=False,
    )
```

```python
import functools

import jax
import jax.numpy as jnp
from jax import lax
from jax.experimental import pallas as pl
from jax.experimental.pallas import tpu as pltpu
from jax.sharding import Mesh
from jax.sharding import PartitionSpec as P

CH = 16
HH = 64
WW = 64
ITERS = 4
LANES = 128


blur = 0.1


def sinkhorn_kernel(scale, cross_ref, noise_ref, coupled_ref):
    scores = cross_ref[...] * scale
    col = jnp.zeros((1, scores.shape[1]), jnp.float32)
    for step in range(ITERS):
        shifted = scores + col
        top = jnp.max(shifted, axis=1, keepdims=True)
        total = jnp.sum(jnp.exp(shifted - top), axis=1, keepdims=True)
        row = -(top + jnp.log(total))
        shifted = scores + row
        top = jnp.max(shifted, axis=0, keepdims=True)
        total = jnp.sum(jnp.exp(shifted - top), axis=0, keepdims=True)
        col = -(top + jnp.log(total))
    shifted = scores + col
    top = jnp.max(shifted, axis=1, keepdims=True)
    grown = jnp.exp(shifted - top)
    weights = (grown / jnp.sum(grown, axis=1, keepdims=True)).astype(jnp.bfloat16)
    coupled_ref[...] = jnp.dot(weights, noise_ref[...], preferred_element_type=jnp.float32)


def patch_rows(moved):
    chans, rows, wide = moved.shape
    strips = wide // LANES
    per = LANES // 4
    to = lax.broadcasted_iota(jnp.int32, (LANES, LANES), 0)
    come = lax.broadcasted_iota(jnp.int32, (LANES, LANES), 1)
    order = (come == to // (2 * per) * (2 * per) + to % per * 2 + to // per % 2).astype(jnp.bfloat16)
    flat = moved.reshape(chans * rows, wide)
    strip = []
    for p in range(strips):
        t = lax.dot_general(order, flat[:, p * LANES:(p + 1) * LANES], (((1,), (1,)), ((), ())),
                            preferred_element_type=jnp.float32).astype(jnp.bfloat16)
        strip.append(jnp.concatenate([t[f * per:(f + 1) * per] for f in range(4)], axis=1))
    strip = jnp.concatenate(strip, axis=0)
    k = strip.shape[1]
    come = lax.broadcasted_iota(jnp.int32, (k, k), 0)
    to = lax.broadcasted_iota(jnp.int32, (k, k), 1)
    f, c, r = come // (chans * rows), come // rows % chans, come % rows
    place = (to == r * (4 * chans) + c * 4 + f).astype(jnp.bfloat16)
    return jnp.dot(strip, place, preferred_element_type=jnp.float32).astype(jnp.bfloat16)

def a_kernel(tn, tm, side_ref, moved_ref, wp_ref, bias_ref, gain_ref, w_hbm, qkv_hbm, normed_hbm,
             w_buf, out_buf, normed, w_sem, out_sem, n_sem):
    tiles = w_hbm.shape[1] // tn
    ins = [pltpu.make_async_copy(w_hbm.at[:, pl.ds(t * tn, tn)], w_buf.at[t], w_sem.at[t]) for t in range(tiles)]
    for c in ins: c.start()
    chans, rows, wide = moved_ref.shape
    tok = wide // 4
    feat = 4 * chans
    x = patch_rows(moved_ref[...])
    for r in range(rows):
        embed = jnp.dot(x[:, r * feat:(r + 1) * feat], wp_ref[...], preferred_element_type=jnp.float32) + bias_ref[...][None, :]
        center = embed - jnp.mean(embed, axis=1, keepdims=True)
        spread = jnp.mean(center * center, axis=1, keepdims=True)
        normed[r * tok:(r + 1) * tok, :] = (center * lax.rsqrt(spread + 1e-05) * gain_ref[...][None, :]).astype(jnp.bfloat16)
    ncopy = pltpu.make_async_copy(normed, normed_hbm, n_sem)
    ncopy.start()
    matmul(tn, tm, side_ref[0] * tiles, ins, normed, w_buf, out_buf, qkv_hbm, out_sem)
    ncopy.wait()

def matmul(tn, tm, first, ins, normed, w_buf, out_buf, qkv_hbm, out_sem):
    n_tok = normed.shape[0]
    outs = []
    for t in range(len(ins)):
        ins[t].wait()
        for m in range(0, n_tok, tm):
            out_buf[t, m:m + tm, :] = jnp.dot(normed[m:m + tm, :], w_buf[t], preferred_element_type=jnp.float32).astype(jnp.bfloat16)
        col = pl.multiple_of((first + t) * tn, tn)
        c = pltpu.make_async_copy(out_buf.at[t], qkv_hbm.at[:, pl.ds(col, tn)], out_sem.at[t])
        c.start()
        outs.append(c)
    for c in outs: c.wait()

def b_kernel(tn, tm, side_ref, normed_hbm, w_hbm, old, qkv_hbm, w_buf, out_buf, normed, w_sem, out_sem, n_sem):
    tiles = w_hbm.shape[1] // tn
    ncopy = pltpu.make_async_copy(normed_hbm, normed, n_sem)
    ncopy.start()
    ins = [pltpu.make_async_copy(w_hbm.at[:, pl.ds(t * tn, tn)], w_buf.at[t], w_sem.at[t]) for t in range(tiles)]
    for c in ins: c.start()
    ncopy.wait()
    matmul(tn, tm, (1 - side_ref[0]) * tiles, ins, normed, w_buf, out_buf, qkv_hbm, out_sem)

def scratch(hid, half, n_tok, tn):
    t = half // tn
    return [pltpu.VMEM((t, hid, tn), jnp.bfloat16), pltpu.VMEM((t, n_tok, tn), jnp.bfloat16), pltpu.VMEM((n_tok, hid), jnp.bfloat16),
            pltpu.SemaphoreType.DMA((t,)), pltpu.SemaphoreType.DMA((t,)), pltpu.SemaphoreType.DMA]

def first_half(side, moved, w_patch, bias, gain, w_half, tn, tm):
    chans, rows, wide = moved.shape
    n_tok = rows * wide // 4
    hid, half = w_half.shape
    vm = pl.BlockSpec(memory_space=pltpu.VMEM)
    anym = pl.BlockSpec(memory_space=pl.ANY)
    return pl.pallas_call(
        functools.partial(a_kernel, tn, tm),
        in_specs=[pl.BlockSpec(memory_space=pltpu.SMEM), vm, vm, vm, vm, anym],
        out_specs=[anym, anym],
        out_shape=[jax.ShapeDtypeStruct((n_tok, 2 * half), jnp.bfloat16), jax.ShapeDtypeStruct((n_tok, hid), jnp.bfloat16)],
        scratch_shapes=scratch(hid, half, n_tok, tn),
        compiler_params=pltpu.CompilerParams(vmem_limit_bytes=48 * 2**20),
        cost_estimate=pl.CostEstimate(flops=2 * n_tok * hid * half, bytes_accessed=2 * hid * half, transcendentals=0),
    )(side, moved, w_patch, bias, gain, w_half)

def second_half(side, normed, w_half, qkv, tn, tm):
    n_tok, hid = normed.shape
    half = w_half.shape[1]
    anym = pl.BlockSpec(memory_space=pl.ANY)
    return pl.pallas_call(
        functools.partial(b_kernel, tn, tm),
        in_specs=[pl.BlockSpec(memory_space=pltpu.SMEM), anym, anym, anym],
        out_specs=anym,
        out_shape=jax.ShapeDtypeStruct(qkv.shape, jnp.bfloat16),
        input_output_aliases={3: 0},
        scratch_shapes=scratch(hid, half, n_tok, tn),
        compiler_params=pltpu.CompilerParams(vmem_limit_bytes=48 * 2**20),
        cost_estimate=pl.CostEstimate(flops=2 * n_tok * hid * half, bytes_accessed=2 * hid * half, transcendentals=0),
    )(side, normed, w_half, qkv)


def per_device(data, noise, times, w_patch, patch_bias, norm_gain, w_qkv):
    row_count, val_width = data.shape
    dp_devices = lax.axis_size("dp")
    val = ("x", "core")
    val_devices = lax.axis_size(val)
    rows = row_count * dp_devices
    part = val_width // dp_devices
    everyone = ("dp", "x", "core")
    local_chan = CH // val_devices
    strip = HH // val_devices * WW
    pieces = strip // part
    half = w_qkv.shape[1] // 2
    side = lax.axis_index("core")
    w_own = lax.dynamic_slice_in_dim(w_qkv, side * half, half, axis=1)
    w_own = lax.all_gather(w_own, "dp", axis=0, tiled=True)
    w_other = lax.ppermute(w_own, "core", [(0, 1), (1, 0)])
    pair = jnp.concatenate([data, noise], axis=0)
    pair = jnp.transpose(pair.reshape(2 * row_count, dp_devices, part), (1, 0, 2))
    pair = lax.all_to_all(pair, "dp", split_axis=0, concat_axis=0, tiled=True)
    data_part = pair[:, :row_count].reshape(rows, part)
    noise_part = pair[:, row_count:].reshape(rows, part)
    cross = lax.dot_general(
        data_part, noise_part, (((1,), (1,)), ((), ())), preferred_element_type=jnp.float32
    )
    cross = cross.reshape(rows, rows // LANES, LANES)
    cross = lax.all_to_all(cross, everyone, split_axis=0, concat_axis=0, tiled=True)
    own = jnp.sum(cross, axis=0, keepdims=True)
    own = jnp.broadcast_to(own, (rows, rows // LANES, LANES))
    cross = lax.all_to_all(own, everyone, split_axis=0, concat_axis=0, tiled=True)
    cross = cross.reshape(rows, rows)
    scale = 1.0 / (float(val_width * val_devices) ** 0.5 * blur)
    coupled = pl.pallas_call(
        functools.partial(sinkhorn_kernel, scale),
        out_shape=jax.ShapeDtypeStruct((rows, part), jnp.float32),
        in_specs=[pl.BlockSpec(memory_space=pltpu.VMEM)] * 2,
        out_specs=pl.BlockSpec(memory_space=pltpu.VMEM),
        compiler_params=pltpu.CompilerParams(vmem_limit_bytes=16 * 2**20),
    )(cross, noise_part)
    coupled = coupled.reshape(dp_devices, row_count, part)
    coupled = lax.all_to_all(coupled, "dp", split_axis=0, concat_axis=0, tiled=True)
    own_data = jnp.transpose(data.reshape(row_count, dp_devices, part), (1, 0, 2)).astype(jnp.float32)
    blend = times[None, :, None]
    mixed = ((1.0 - blend) * coupled + blend * own_data).astype(jnp.bfloat16)
    target = (own_data - coupled).astype(jnp.bfloat16)
    target = jnp.transpose(target, (1, 0, 2)).reshape(row_count, val_width)
    mixed = mixed.reshape(local_chan, val_devices, pieces, row_count, part)
    mixed = jnp.transpose(mixed, (1, 0, 3, 2, 4)).reshape(val_devices, local_chan, row_count, strip)
    moved = lax.all_to_all(mixed, val, split_axis=0, concat_axis=0, tiled=True)
    moved = moved.reshape(CH, row_count, strip)
    side = side.astype(jnp.int32).reshape(1)
    qkv, normed = first_half(side, moved, w_patch, patch_bias, norm_gain, w_own, 768, 256)
    qkv = second_half(side, normed, w_other, qkv, 768, 256)
    return (qkv.reshape(row_count, -1, 2 * half), target)


def solution(mesh):
    devices = mesh.devices
    fine = Mesh(devices.reshape(devices.shape[0], -1, 2), ("dp", "x", "core"))
    val = ("x", "core")
    return jax.shard_map(
        per_device,
        mesh=fine,
        in_specs=(P("dp", val), P("dp", val), P("dp"), P(), P(), P(), P("dp", None)),
        out_specs=(P("dp", val, None), P("dp", val)),
        check_vma=False,
    )
```

```python
import functools

import jax
import jax.numpy as jnp
from jax import lax
from jax.experimental import pallas as pl
from jax.experimental.pallas import tpu as pltpu
from jax.sharding import Mesh
from jax.sharding import PartitionSpec as P

CH = 16
HH = 64
WW = 64
ITERS = 4
LANES = 128


blur = 0.1


def sinkhorn_kernel(scale, cross_ref, noise_ref, coupled_ref):
    scores = cross_ref[...] * scale
    col = jnp.zeros((1, scores.shape[1]), jnp.float32)
    for step in range(ITERS):
        shifted = scores + col
        top = jnp.max(shifted, axis=1, keepdims=True)
        total = jnp.sum(jnp.exp(shifted - top), axis=1, keepdims=True)
        row = -(top + jnp.log(total))
        shifted = scores + row
        top = jnp.max(shifted, axis=0, keepdims=True)
        total = jnp.sum(jnp.exp(shifted - top), axis=0, keepdims=True)
        col = -(top + jnp.log(total))
    shifted = scores + col
    top = jnp.max(shifted, axis=1, keepdims=True)
    grown = jnp.exp(shifted - top)
    weights = (grown / jnp.sum(grown, axis=1, keepdims=True)).astype(jnp.bfloat16)
    coupled_ref[...] = jnp.dot(weights, noise_ref[...], preferred_element_type=jnp.float32)


def patch_rows(moved):
    chans, rows, wide = moved.shape
    strips = wide // LANES
    per = LANES // 4
    to = lax.broadcasted_iota(jnp.int32, (LANES, LANES), 0)
    come = lax.broadcasted_iota(jnp.int32, (LANES, LANES), 1)
    order = (come == to // (2 * per) * (2 * per) + to % per * 2 + to // per % 2).astype(jnp.bfloat16)
    flat = moved.reshape(chans * rows, wide)
    strip = []
    for p in range(strips):
        t = lax.dot_general(order, flat[:, p * LANES:(p + 1) * LANES], (((1,), (1,)), ((), ())),
                            preferred_element_type=jnp.float32).astype(jnp.bfloat16)
        strip.append(jnp.concatenate([t[f * per:(f + 1) * per] for f in range(4)], axis=1))
    strip = jnp.concatenate(strip, axis=0)
    k = strip.shape[1]
    come = lax.broadcasted_iota(jnp.int32, (k, k), 0)
    to = lax.broadcasted_iota(jnp.int32, (k, k), 1)
    f, c, r = come // (chans * rows), come // rows % chans, come % rows
    place = (to == r * (4 * chans) + c * 4 + f).astype(jnp.bfloat16)
    return jnp.dot(strip, place, preferred_element_type=jnp.float32).astype(jnp.bfloat16)

def a_kernel(tn, tm, side_ref, moved_ref, wp_ref, bias_ref, gain_ref, w_hbm, qkv_hbm, normed_hbm,
             w_buf, out_buf, normed, w_sem, out_sem, n_sem):
    tiles = w_hbm.shape[1] // tn
    ins = [pltpu.make_async_copy(w_hbm.at[:, pl.ds(t * tn, tn)], w_buf.at[t], w_sem.at[t]) for t in range(tiles)]
    for c in ins: c.start()
    chans, rows, wide = moved_ref.shape
    tok = wide // 4
    feat = 4 * chans
    x = patch_rows(moved_ref[...])
    for r in range(rows):
        embed = jnp.dot(x[:, r * feat:(r + 1) * feat], wp_ref[...], preferred_element_type=jnp.float32) + bias_ref[...][None, :]
        center = embed - jnp.mean(embed, axis=1, keepdims=True)
        spread = jnp.mean(center * center, axis=1, keepdims=True)
        normed[r * tok:(r + 1) * tok, :] = (center * lax.rsqrt(spread + 1e-05) * gain_ref[...][None, :]).astype(jnp.bfloat16)
    ncopy = pltpu.make_async_copy(normed, normed_hbm, n_sem)
    ncopy.start()
    matmul(tn, tm, side_ref[0] * tiles, ins, normed, w_buf, out_buf, qkv_hbm, out_sem)
    ncopy.wait()

def matmul(tn, tm, first, ins, normed, w_buf, out_buf, qkv_hbm, out_sem):
    n_tok = normed.shape[0]
    outs = []
    for t in range(len(ins)):
        ins[t].wait()
        for m in range(0, n_tok, tm):
            out_buf[t, m:m + tm, :] = jnp.dot(normed[m:m + tm, :], w_buf[t], preferred_element_type=jnp.float32).astype(jnp.bfloat16)
        col = pl.multiple_of((first + t) * tn, tn)
        c = pltpu.make_async_copy(out_buf.at[t], qkv_hbm.at[:, pl.ds(col, tn)], out_sem.at[t])
        c.start()
        outs.append(c)
    for c in outs: c.wait()

def b_kernel(tn, tm, side_ref, normed_hbm, w_hbm, old, qkv_hbm, w_buf, out_buf, normed, w_sem, out_sem, n_sem):
    tiles = w_hbm.shape[1] // tn
    ncopy = pltpu.make_async_copy(normed_hbm, normed, n_sem)
    ncopy.start()
    ins = [pltpu.make_async_copy(w_hbm.at[:, pl.ds(t * tn, tn)], w_buf.at[t], w_sem.at[t]) for t in range(tiles)]
    for c in ins: c.start()
    ncopy.wait()
    matmul(tn, tm, (1 - side_ref[0]) * tiles, ins, normed, w_buf, out_buf, qkv_hbm, out_sem)

def scratch(hid, half, n_tok, tn):
    t = half // tn
    return [pltpu.VMEM((t, hid, tn), jnp.bfloat16), pltpu.VMEM((t, n_tok, tn), jnp.bfloat16), pltpu.VMEM((n_tok, hid), jnp.bfloat16),
            pltpu.SemaphoreType.DMA((t,)), pltpu.SemaphoreType.DMA((t,)), pltpu.SemaphoreType.DMA]

def first_half(side, moved, w_patch, bias, gain, w_half, tn, tm):
    chans, rows, wide = moved.shape
    n_tok = rows * wide // 4
    hid, half = w_half.shape
    vm = pl.BlockSpec(memory_space=pltpu.VMEM)
    anym = pl.BlockSpec(memory_space=pl.ANY)
    return pl.pallas_call(
        functools.partial(a_kernel, tn, tm),
        in_specs=[pl.BlockSpec(memory_space=pltpu.SMEM), vm, vm, vm, vm, anym],
        out_specs=[anym, anym],
        out_shape=[jax.ShapeDtypeStruct((n_tok, 2 * half), jnp.bfloat16), jax.ShapeDtypeStruct((n_tok, hid), jnp.bfloat16)],
        scratch_shapes=scratch(hid, half, n_tok, tn),
        compiler_params=pltpu.CompilerParams(vmem_limit_bytes=48 * 2**20),
        cost_estimate=pl.CostEstimate(flops=2 * n_tok * hid * half, bytes_accessed=2 * hid * half, transcendentals=0),
    )(side, moved, w_patch, bias, gain, w_half)

def second_half(side, normed, w_half, qkv, tn, tm):
    n_tok, hid = normed.shape
    half = w_half.shape[1]
    anym = pl.BlockSpec(memory_space=pl.ANY)
    return pl.pallas_call(
        functools.partial(b_kernel, tn, tm),
        in_specs=[pl.BlockSpec(memory_space=pltpu.SMEM), anym, anym, anym],
        out_specs=anym,
        out_shape=jax.ShapeDtypeStruct(qkv.shape, jnp.bfloat16),
        input_output_aliases={3: 0},
        scratch_shapes=scratch(hid, half, n_tok, tn),
        compiler_params=pltpu.CompilerParams(vmem_limit_bytes=48 * 2**20),
        cost_estimate=pl.CostEstimate(flops=2 * n_tok * hid * half, bytes_accessed=2 * hid * half, transcendentals=0),
    )(side, normed, w_half, qkv)


def per_device(data, noise, times, w_patch, patch_bias, norm_gain, w_qkv):
    row_count, val_width = data.shape
    dp_devices = lax.axis_size("dp")
    val = ("x", "core")
    val_devices = lax.axis_size(val)
    rows = row_count * dp_devices
    part = val_width // dp_devices
    everyone = ("dp", "x", "core")
    local_chan = CH // val_devices
    strip = HH // val_devices * WW
    pieces = strip // part
    half = w_qkv.shape[1] // 2
    side = lax.axis_index("core")
    w_own = lax.dynamic_slice_in_dim(w_qkv, side * half, half, axis=1)
    w_own = lax.all_gather(w_own, "dp", axis=0, tiled=True)
    pair = jnp.concatenate([data, noise], axis=0)
    pair = jnp.transpose(pair.reshape(2 * row_count, dp_devices, part), (1, 0, 2))
    pair = lax.all_to_all(pair, "dp", split_axis=0, concat_axis=0, tiled=True)
    data_part = pair[:, :row_count].reshape(rows, part)
    noise_part = pair[:, row_count:].reshape(rows, part)
    cross = lax.dot_general(
        data_part, noise_part, (((1,), (1,)), ((), ())), preferred_element_type=jnp.float32
    )
    cross = cross.reshape(rows, rows // LANES, LANES)
    cross = lax.all_to_all(cross, everyone, split_axis=0, concat_axis=0, tiled=True)
    own = jnp.sum(cross, axis=0, keepdims=True)
    own = jnp.broadcast_to(own, (rows, rows // LANES, LANES))
    cross = lax.all_to_all(own, everyone, split_axis=0, concat_axis=0, tiled=True)
    cross = cross.reshape(rows, rows)
    scale = 1.0 / (float(val_width * val_devices) ** 0.5 * blur)
    coupled = pl.pallas_call(
        functools.partial(sinkhorn_kernel, scale),
        out_shape=jax.ShapeDtypeStruct((rows, part), jnp.float32),
        in_specs=[pl.BlockSpec(memory_space=pltpu.VMEM)] * 2,
        out_specs=pl.BlockSpec(memory_space=pltpu.VMEM),
        compiler_params=pltpu.CompilerParams(vmem_limit_bytes=16 * 2**20),
    )(cross, noise_part)
    coupled = coupled.reshape(dp_devices, row_count, part)
    coupled = lax.all_to_all(coupled, "dp", split_axis=0, concat_axis=0, tiled=True)
    own_data = jnp.transpose(data.reshape(row_count, dp_devices, part), (1, 0, 2)).astype(jnp.float32)
    blend = times[None, :, None]
    mixed = ((1.0 - blend) * coupled + blend * own_data).astype(jnp.bfloat16)
    target = (own_data - coupled).astype(jnp.bfloat16)
    target = jnp.transpose(target, (1, 0, 2)).reshape(row_count, val_width)
    mixed = mixed.reshape(local_chan, val_devices, pieces, row_count, part)
    mixed = jnp.transpose(mixed, (1, 0, 3, 2, 4)).reshape(val_devices, local_chan, row_count, strip)
    moved = lax.all_to_all(mixed, val, split_axis=0, concat_axis=0, tiled=True)
    moved, w_own = lax.optimization_barrier((moved, w_own))
    w_other = lax.ppermute(w_own, "core", [(0, 1), (1, 0)])
    moved = moved.reshape(CH, row_count, strip)
    side = side.astype(jnp.int32).reshape(1)
    qkv, normed = first_half(side, moved, w_patch, patch_bias, norm_gain, w_own, 768, 256)
    qkv = second_half(side, normed, w_other, qkv, 768, 256)
    return (qkv.reshape(row_count, -1, 2 * half), target)


def solution(mesh):
    devices = mesh.devices
    fine = Mesh(devices.reshape(devices.shape[0], -1, 2), ("dp", "x", "core"))
    val = ("x", "core")
    return jax.shard_map(
        per_device,
        mesh=fine,
        in_specs=(P("dp", val), P("dp", val), P("dp"), P(), P(), P(), P("dp", None)),
        out_specs=(P("dp", val, None), P("dp", val)),
        check_vma=False,
    )
```

```python
import functools

import jax
import jax.numpy as jnp
from jax import lax
from jax.experimental import pallas as pl
from jax.experimental.pallas import tpu as pltpu
from jax.sharding import Mesh
from jax.sharding import PartitionSpec as P

CH = 16
HH = 64
WW = 64
ITERS = 4
LANES = 128


blur = 0.1


def share_kernel(side_ref, times_ref, parts_ref, out_ref):
    own = jnp.sum(parts_ref[...], axis=0, keepdims=True)
    own = own - own[:, :1, :1]
    first = lax.broadcasted_iota(jnp.int32, own.shape, 1) + lax.broadcasted_iota(jnp.int32, own.shape, 2) == 0
    own = jnp.where(first, times_ref[side_ref[0]], own)
    out_ref[...] = jnp.broadcast_to(own, out_ref.shape)


def sinkhorn_kernel(scale, cross_ref, data_ref, noise_ref, moved_ref, out_ref):
    rows, part = data_ref.shape
    cross = cross_ref[...]
    blend = cross[:, :1]
    cross = jnp.where(lax.broadcasted_iota(jnp.int32, cross.shape, 1) == 0, 0.0, cross)
    scores = cross * scale
    col = jnp.zeros((1, scores.shape[1]), jnp.float32)
    for step in range(ITERS):
        shifted = scores + col
        top = jnp.max(shifted, axis=1, keepdims=True)
        total = jnp.sum(jnp.exp(shifted - top), axis=1, keepdims=True)
        row = -(top + jnp.log(total))
        shifted = scores + row
        top = jnp.max(shifted, axis=0, keepdims=True)
        total = jnp.sum(jnp.exp(shifted - top), axis=0, keepdims=True)
        col = -(top + jnp.log(total))
    shifted = scores + col
    top = jnp.max(shifted, axis=1, keepdims=True)
    grown = jnp.exp(shifted - top)
    weights = (grown / jnp.sum(grown, axis=1, keepdims=True)).astype(jnp.bfloat16)
    coupled = jnp.dot(weights, noise_ref[...], preferred_element_type=jnp.float32)
    target = data_ref[...].astype(jnp.float32) - coupled
    moved = moved_ref[...].astype(jnp.float32)
    group = moved.shape[1] // 2
    moved_data = moved[:, :group].reshape(rows, part)
    moved_noise = moved[:, group:].reshape(rows, part).astype(jnp.bfloat16)
    coupled = jnp.dot(weights, moved_noise, preferred_element_type=jnp.float32)
    mixed = (1.0 - blend) * coupled + blend * moved_data
    both = [mixed.reshape(-1, group, part), target.reshape(-1, group, part)]
    out_ref[...] = jnp.concatenate(both, axis=1).astype(jnp.bfloat16)


def patch_rows(moved):
    chans, pieces, rows, part = moved.shape
    strips = pieces * part // LANES
    per = LANES // 4
    to = lax.broadcasted_iota(jnp.int32, (LANES, LANES), 0)
    come = lax.broadcasted_iota(jnp.int32, (LANES, LANES), 1)
    order = (come == to // (2 * per) * (2 * per) + to % per * 2 + to // per % 2).astype(jnp.bfloat16)
    flat = [moved[:, h].reshape(chans * rows, part) for h in range(pieces)]
    strip = []
    for p in range(strips):
        at = p * LANES % part
        t = lax.dot_general(order, flat[p * LANES // part][:, at:at + LANES], (((1,), (1,)), ((), ())),
                            preferred_element_type=jnp.float32).astype(jnp.bfloat16)
        strip.append(jnp.concatenate([t[f * per:(f + 1) * per] for f in range(4)], axis=1))
    strip = jnp.concatenate(strip, axis=0)
    k = strip.shape[1]
    come = lax.broadcasted_iota(jnp.int32, (k, k), 0)
    to = lax.broadcasted_iota(jnp.int32, (k, k), 1)
    f, c, r = come // (chans * rows), come // rows % chans, come % rows
    place = (to == r * (4 * chans) + c * 4 + f).astype(jnp.bfloat16)
    return jnp.dot(strip, place, preferred_element_type=jnp.float32).astype(jnp.bfloat16)

def a_kernel(tn, tm, side_ref, moved_ref, wp_ref, bias_ref, gain_ref, w_hbm, qkv_hbm, normed,
             w_buf, out_buf, w_sem, out_sem):
    tiles = w_hbm.shape[1] // tn
    ins = [pltpu.make_async_copy(w_hbm.at[:, pl.ds(t * tn, tn)], w_buf.at[t], w_sem.at[t]) for t in range(tiles)]
    for c in ins: c.start()
    chans, pieces, rows, part = moved_ref.shape
    tok = pieces * part // 4
    feat = 4 * chans
    x = patch_rows(moved_ref[...])
    for r in range(rows):
        embed = jnp.dot(x[:, r * feat:(r + 1) * feat], wp_ref[...], preferred_element_type=jnp.float32) + bias_ref[...][None, :]
        center = embed - jnp.mean(embed, axis=1, keepdims=True)
        spread = jnp.mean(center * center, axis=1, keepdims=True)
        normed[r * tok:(r + 1) * tok, :] = (center * lax.rsqrt(spread + 1e-05) * gain_ref[...][None, :]).astype(jnp.bfloat16)
    first = side_ref[0] * tiles
    matmul(tn, tm, first, lambda t: w_buf.at[t], ins, normed, out_buf, qkv_hbm, out_sem)


def matmul(tn, tm, first, w_tile, ins, normed, out_buf, qkv_hbm, out_sem):
    n_tok = normed.shape[0]
    tiles = out_buf.shape[0]
    outs = []
    for t in range(tiles):
        if ins:
            ins[t].wait()
        w = w_tile(t)
        for m in range(0, n_tok, tm):
            out_buf[t, m:m + tm, :] = jnp.dot(
                normed[m:m + tm, :], w[...], preferred_element_type=jnp.float32
            ).astype(jnp.bfloat16)
        col = pl.multiple_of((first + t) * tn, tn)
        copy = pltpu.make_async_copy(out_buf.at[t], qkv_hbm.at[:, pl.ds(col, tn)], out_sem.at[t])
        copy.start()
        outs.append(copy)
    for copy in outs:
        copy.wait()


def b_kernel(tn, tm, side_ref, normed, w_ref, old, qkv_hbm, out_buf, out_sem):
    tiles = out_buf.shape[0]
    first = (1 - side_ref[0]) * tiles
    matmul(tn, tm, first, lambda t: w_ref.at[:, t * tn:(t + 1) * tn], None, normed, out_buf, qkv_hbm, out_sem)


def first_half(side, moved, w_patch, bias, gain, w_half, tn, tm):
    chans, pieces, rows, part = moved.shape
    n_tok = rows * pieces * part // 4
    hid, half = w_half.shape
    tiles = half // tn
    vm = pl.BlockSpec(memory_space=pltpu.VMEM)
    anym = pl.BlockSpec(memory_space=pl.ANY)
    return pl.pallas_call(
        functools.partial(a_kernel, tn, tm),
        in_specs=[pl.BlockSpec(memory_space=pltpu.SMEM), vm, vm, vm, vm, anym],
        out_specs=[anym, vm],
        out_shape=[
            jax.ShapeDtypeStruct((n_tok, 2 * half), jnp.bfloat16),
            jax.ShapeDtypeStruct((n_tok, hid), jnp.bfloat16),
        ],
        scratch_shapes=[
            pltpu.VMEM((tiles, hid, tn), jnp.bfloat16),
            pltpu.VMEM((tiles, n_tok, tn), jnp.bfloat16),
            pltpu.SemaphoreType.DMA((tiles,)),
            pltpu.SemaphoreType.DMA((tiles,)),
        ],
        compiler_params=pltpu.CompilerParams(vmem_limit_bytes=48 * 2**20),
        cost_estimate=pl.CostEstimate(flops=2 * n_tok * hid * half, bytes_accessed=2 * hid * half, transcendentals=0),
    )(side, moved, w_patch, bias, gain, w_half)


def second_half(side, normed, w_half, qkv, tn, tm):
    n_tok, hid = normed.shape
    half = w_half.shape[1]
    tiles = half // tn
    vm = pl.BlockSpec(memory_space=pltpu.VMEM)
    anym = pl.BlockSpec(memory_space=pl.ANY)
    return pl.pallas_call(
        functools.partial(b_kernel, tn, tm),
        in_specs=[pl.BlockSpec(memory_space=pltpu.SMEM), vm, vm, anym],
        out_specs=anym,
        out_shape=jax.ShapeDtypeStruct(qkv.shape, jnp.bfloat16),
        input_output_aliases={3: 0},
        scratch_shapes=[pltpu.VMEM((tiles, n_tok, tn), jnp.bfloat16), pltpu.SemaphoreType.DMA((tiles,))],
        compiler_params=pltpu.CompilerParams(vmem_limit_bytes=44 * 2**20),
        cost_estimate=pl.CostEstimate(flops=2 * n_tok * hid * half, bytes_accessed=2 * hid * half, transcendentals=0),
    )(side, normed, w_half, qkv)


def per_device(data, noise, times, w_patch, patch_bias, norm_gain, w_qkv):
    row_count, val_width = data.shape
    dp_devices = lax.axis_size("dp")
    val = ("x", "core")
    val_devices = lax.axis_size(val)
    rows = row_count * dp_devices
    part = val_width // dp_devices
    everyone = ("dp", "x", "core")
    local_chan = CH // val_devices
    strip = HH // val_devices * WW
    pieces = strip // part
    half = w_qkv.shape[1] // 2
    side = lax.axis_index("core")
    w_own = lax.dynamic_slice_in_dim(w_qkv, side * half, half, axis=1)
    w_own = lax.all_gather(w_own, "dp", axis=0, tiled=True)
    pair = jnp.concatenate([data, noise], axis=0)
    pair = jnp.transpose(pair.reshape(2 * row_count, dp_devices, part), (1, 0, 2))
    pair = lax.all_to_all(pair, "dp", split_axis=0, concat_axis=0, tiled=True)
    route = []
    for d in range(dp_devices):
        chan, block, piece = d // (val_devices * pieces), d // pieces % val_devices, d % pieces
        for v in range(val_devices):
            to = (v * local_chan + chan) * pieces + piece
            route.append((d * val_devices + v, to * val_devices + block))
    moved = lax.ppermute(pair, everyone, route)
    data_part = pair[:, :row_count].reshape(rows, part)
    noise_part = pair[:, row_count:].reshape(rows, part)
    cross = lax.dot_general(
        data_part, noise_part, (((1,), (1,)), ((), ())), preferred_element_type=jnp.float32
    )
    cross = cross.reshape(rows, rows // LANES, LANES)
    cross = lax.all_to_all(cross, everyone, split_axis=0, concat_axis=0, tiled=True)
    v = lax.axis_index(val).astype(jnp.int32).reshape(1)
    vm = pl.BlockSpec(memory_space=pltpu.VMEM)
    sm = pl.BlockSpec(memory_space=pltpu.SMEM)
    cross = pl.pallas_call(
        share_kernel,
        out_shape=jax.ShapeDtypeStruct(cross.shape, jnp.float32),
        in_specs=[sm, sm, vm],
        out_specs=vm,
    )(v, times, cross)
    cross = lax.all_to_all(cross, everyone, split_axis=0, concat_axis=0, tiled=True)
    cross = cross.reshape(rows, rows)
    scale = 1.0 / (float(val_width * val_devices) ** 0.5 * blur)
    both = pl.pallas_call(
        functools.partial(sinkhorn_kernel, scale),
        out_shape=jax.ShapeDtypeStruct(pair.shape, jnp.bfloat16),
        in_specs=[vm] * 4,
        out_specs=vm,
        compiler_params=pltpu.CompilerParams(vmem_limit_bytes=16 * 2**20),
    )(cross, data_part, noise_part, moved)
    both = lax.all_to_all(both, "dp", split_axis=0, concat_axis=0, tiled=True)
    target = jnp.transpose(both[:, row_count:], (1, 0, 2)).reshape(row_count, val_width)
    mixed = both[:, :row_count].reshape(CH, pieces, row_count, part)
    mixed, w_own = lax.optimization_barrier((mixed, w_own))
    w_other = lax.ppermute(w_own, "core", [(0, 1), (1, 0)])
    side = side.astype(jnp.int32).reshape(1)
    qkv, normed = first_half(side, mixed, w_patch, patch_bias, norm_gain, w_own, 768, 256)
    qkv = second_half(side, normed, w_other, qkv, 768, 256)
    return (qkv.reshape(row_count, -1, 2 * half), target)


def solution(mesh):
    devices = mesh.devices
    fine = Mesh(devices.reshape(devices.shape[0], -1, 2), ("dp", "x", "core"))
    val = ("x", "core")
    return jax.shard_map(
        per_device,
        mesh=fine,
        in_specs=(P("dp", val), P("dp", val), P("dp"), P(), P(), P(), P("dp", None)),
        out_specs=(P("dp", val, None), P("dp", val)),
        check_vma=False,
    )
```

```python
import functools

import jax
import jax.numpy as jnp
from jax import lax
from jax.experimental import pallas as pl
from jax.experimental.pallas import tpu as pltpu
from jax.sharding import Mesh
from jax.sharding import PartitionSpec as P

CH = 16
HH = 64
WW = 64
ITERS = 4
LANES = 128


blur = 0.1


def sinkhorn_kernel(scale, cross_ref, noise_ref, coupled_ref):
    scores = cross_ref[...] * scale
    col = jnp.zeros((1, scores.shape[1]), jnp.float32)
    for step in range(ITERS):
        shifted = scores + col
        top = jnp.max(shifted, axis=1, keepdims=True)
        total = jnp.sum(jnp.exp(shifted - top), axis=1, keepdims=True)
        row = -(top + jnp.log(total))
        shifted = scores + row
        top = jnp.max(shifted, axis=0, keepdims=True)
        total = jnp.sum(jnp.exp(shifted - top), axis=0, keepdims=True)
        col = -(top + jnp.log(total))
    shifted = scores + col
    top = jnp.max(shifted, axis=1, keepdims=True)
    grown = jnp.exp(shifted - top)
    weights = (grown / jnp.sum(grown, axis=1, keepdims=True)).astype(jnp.bfloat16)
    coupled_ref[...] = jnp.dot(weights, noise_ref[...], preferred_element_type=jnp.float32)


def patch_rows(moved):
    chans, rows, wide = moved.shape
    strips = wide // LANES
    per = LANES // 4
    to = lax.broadcasted_iota(jnp.int32, (LANES, LANES), 0)
    come = lax.broadcasted_iota(jnp.int32, (LANES, LANES), 1)
    order = (come == to // (2 * per) * (2 * per) + to % per * 2 + to // per % 2).astype(jnp.bfloat16)
    flat = moved.reshape(chans * rows, wide)
    strip = []
    for p in range(strips):
        t = lax.dot_general(order, flat[:, p * LANES:(p + 1) * LANES], (((1,), (1,)), ((), ())),
                            preferred_element_type=jnp.float32).astype(jnp.bfloat16)
        strip.append(jnp.concatenate([t[f * per:(f + 1) * per] for f in range(4)], axis=1))
    strip = jnp.concatenate(strip, axis=0)
    k = strip.shape[1]
    come = lax.broadcasted_iota(jnp.int32, (k, k), 0)
    to = lax.broadcasted_iota(jnp.int32, (k, k), 1)
    f, c, r = come // (chans * rows), come // rows % chans, come % rows
    place = (to == r * (4 * chans) + c * 4 + f).astype(jnp.bfloat16)
    return jnp.dot(strip, place, preferred_element_type=jnp.float32).astype(jnp.bfloat16)

def embed_kernel(moved_ref, wp_ref, bias_ref, gain_ref, normed):
    chans, rows, wide = moved_ref.shape
    tok = wide // 4
    feat = 4 * chans
    x = patch_rows(moved_ref[...])
    for r in range(rows):
        embed = jnp.dot(x[:, r * feat:(r + 1) * feat], wp_ref[...], preferred_element_type=jnp.float32) + bias_ref[...][None, :]
        center = embed - jnp.mean(embed, axis=1, keepdims=True)
        spread = jnp.mean(center * center, axis=1, keepdims=True)
        normed[r * tok:(r + 1) * tok, :] = (center * lax.rsqrt(spread + 1e-05) * gain_ref[...][None, :]).astype(jnp.bfloat16)


def a_kernel(tn, tm, side_ref, normed, w_hbm, qkv_hbm, w_buf, out_buf, w_sem, out_sem):
    tiles = w_hbm.shape[1] // tn
    ins = [
        pltpu.make_async_copy(w_hbm.at[:, pl.ds(t * tn, tn)], w_buf.at[t], w_sem.at[t])
        for t in range(tiles)
    ]
    for copy in ins:
        copy.start()
    first = side_ref[0] * tiles
    matmul(tn, tm, first, lambda t: w_buf.at[t], ins, normed, out_buf, qkv_hbm, out_sem)


def matmul(tn, tm, first, w_tile, ins, normed, out_buf, qkv_hbm, out_sem):
    n_tok = normed.shape[0]
    tiles = out_buf.shape[0]
    outs = []
    for t in range(tiles):
        if ins:
            ins[t].wait()
        w = w_tile(t)
        for m in range(0, n_tok, tm):
            out_buf[t, m:m + tm, :] = jnp.dot(
                normed[m:m + tm, :], w[...], preferred_element_type=jnp.float32
            ).astype(jnp.bfloat16)
        col = pl.multiple_of((first + t) * tn, tn)
        copy = pltpu.make_async_copy(out_buf.at[t], qkv_hbm.at[:, pl.ds(col, tn)], out_sem.at[t])
        copy.start()
        outs.append(copy)
    for copy in outs:
        copy.wait()


def b_kernel(tn, tm, side_ref, normed, w_ref, old, qkv_hbm, out_buf, out_sem):
    tiles = out_buf.shape[0]
    first = (1 - side_ref[0]) * tiles
    matmul(tn, tm, first, lambda t: w_ref.at[:, t * tn:(t + 1) * tn], None, normed, out_buf, qkv_hbm, out_sem)


def embed_tokens(moved, w_patch, bias, gain):
    vm = pl.BlockSpec(memory_space=pltpu.VMEM)
    n_tok = moved.size // w_patch.shape[0]
    return pl.pallas_call(
        embed_kernel,
        in_specs=[vm] * 4,
        out_specs=vm,
        out_shape=jax.ShapeDtypeStruct((n_tok, w_patch.shape[1]), jnp.bfloat16),
        compiler_params=pltpu.CompilerParams(vmem_limit_bytes=32 * 2**20),
    )(moved, w_patch, bias, gain)


def first_half(side, normed, w_half, tn, tm):
    n_tok, hid = normed.shape
    half = w_half.shape[1]
    tiles = half // tn
    vm = pl.BlockSpec(memory_space=pltpu.VMEM)
    anym = pl.BlockSpec(memory_space=pl.ANY)
    return pl.pallas_call(
        functools.partial(a_kernel, tn, tm),
        in_specs=[pl.BlockSpec(memory_space=pltpu.SMEM), vm, anym],
        out_specs=anym,
        out_shape=jax.ShapeDtypeStruct((n_tok, 2 * half), jnp.bfloat16),
        scratch_shapes=[
            pltpu.VMEM((tiles, hid, tn), jnp.bfloat16),
            pltpu.VMEM((tiles, n_tok, tn), jnp.bfloat16),
            pltpu.SemaphoreType.DMA((tiles,)),
            pltpu.SemaphoreType.DMA((tiles,)),
        ],
        compiler_params=pltpu.CompilerParams(vmem_limit_bytes=48 * 2**20),
        cost_estimate=pl.CostEstimate(flops=2 * n_tok * hid * half, bytes_accessed=2 * hid * half, transcendentals=0),
    )(side, normed, w_half)


def second_half(side, normed, w_half, qkv, tn, tm):
    n_tok, hid = normed.shape
    half = w_half.shape[1]
    tiles = half // tn
    vm = pl.BlockSpec(memory_space=pltpu.VMEM)
    anym = pl.BlockSpec(memory_space=pl.ANY)
    return pl.pallas_call(
        functools.partial(b_kernel, tn, tm),
        in_specs=[pl.BlockSpec(memory_space=pltpu.SMEM), vm, vm, anym],
        out_specs=anym,
        out_shape=jax.ShapeDtypeStruct(qkv.shape, jnp.bfloat16),
        input_output_aliases={3: 0},
        scratch_shapes=[pltpu.VMEM((tiles, n_tok, tn), jnp.bfloat16), pltpu.SemaphoreType.DMA((tiles,))],
        compiler_params=pltpu.CompilerParams(vmem_limit_bytes=44 * 2**20),
        cost_estimate=pl.CostEstimate(flops=2 * n_tok * hid * half, bytes_accessed=2 * hid * half, transcendentals=0),
    )(side, normed, w_half, qkv)


def per_device(data, noise, times, w_patch, patch_bias, norm_gain, w_qkv):
    row_count, val_width = data.shape
    dp_devices = lax.axis_size("dp")
    val = ("x", "core")
    val_devices = lax.axis_size(val)
    rows = row_count * dp_devices
    part = val_width // dp_devices
    everyone = ("dp", "x", "core")
    local_chan = CH // val_devices
    strip = HH // val_devices * WW
    pieces = strip // part
    half = w_qkv.shape[1] // 2
    side = lax.axis_index("core")
    w_own = lax.dynamic_slice_in_dim(w_qkv, side * half, half, axis=1)
    w_own = lax.all_gather(w_own, "dp", axis=0, tiled=True)
    pair = jnp.concatenate([data, noise], axis=0)
    pair = jnp.transpose(pair.reshape(2 * row_count, dp_devices, part), (1, 0, 2))
    pair = lax.all_to_all(pair, "dp", split_axis=0, concat_axis=0, tiled=True)
    data_part = pair[:, :row_count].reshape(rows, part)
    noise_part = pair[:, row_count:].reshape(rows, part)
    cross = lax.dot_general(
        data_part, noise_part, (((1,), (1,)), ((), ())), preferred_element_type=jnp.float32
    )
    cross = cross.reshape(rows, rows // LANES, LANES)
    cross = lax.all_to_all(cross, everyone, split_axis=0, concat_axis=0, tiled=True)
    own = jnp.sum(cross, axis=0, keepdims=True)
    own = jnp.broadcast_to(own, (rows, rows // LANES, LANES))
    cross = lax.all_to_all(own, everyone, split_axis=0, concat_axis=0, tiled=True)
    cross = cross.reshape(rows, rows)
    scale = 1.0 / (float(val_width * val_devices) ** 0.5 * blur)
    coupled = pl.pallas_call(
        functools.partial(sinkhorn_kernel, scale),
        out_shape=jax.ShapeDtypeStruct((rows, part), jnp.float32),
        in_specs=[pl.BlockSpec(memory_space=pltpu.VMEM)] * 2,
        out_specs=pl.BlockSpec(memory_space=pltpu.VMEM),
        compiler_params=pltpu.CompilerParams(vmem_limit_bytes=16 * 2**20),
    )(cross, noise_part)
    coupled = coupled.reshape(dp_devices, row_count, part)
    coupled = lax.all_to_all(coupled, "dp", split_axis=0, concat_axis=0, tiled=True)
    own_data = jnp.transpose(data.reshape(row_count, dp_devices, part), (1, 0, 2)).astype(jnp.float32)
    blend = times[None, :, None]
    mixed = ((1.0 - blend) * coupled + blend * own_data).astype(jnp.bfloat16)
    target = (own_data - coupled).astype(jnp.bfloat16)
    target = jnp.transpose(target, (1, 0, 2)).reshape(row_count, val_width)
    mixed = mixed.reshape(local_chan, val_devices, pieces, row_count, part)
    mixed = jnp.transpose(mixed, (1, 0, 3, 2, 4)).reshape(val_devices, local_chan, row_count, strip)
    moved = lax.all_to_all(mixed, val, split_axis=0, concat_axis=0, tiled=True)
    moved = moved.reshape(CH, row_count, strip)
    side = side.astype(jnp.int32).reshape(1)
    normed = embed_tokens(moved, w_patch, patch_bias, norm_gain)
    normed, w_own = lax.optimization_barrier((normed, w_own))
    w_other = lax.ppermute(w_own, "core", [(0, 1), (1, 0)])
    qkv = first_half(side, normed, w_own, 768, 256)
    qkv = second_half(side, normed, w_other, qkv, 768, 256)
    return (qkv.reshape(row_count, -1, 2 * half), target)


def solution(mesh):
    devices = mesh.devices
    fine = Mesh(devices.reshape(devices.shape[0], -1, 2), ("dp", "x", "core"))
    val = ("x", "core")
    return jax.shard_map(
        per_device,
        mesh=fine,
        in_specs=(P("dp", val), P("dp", val), P("dp"), P(), P(), P(), P("dp", None)),
        out_specs=(P("dp", val, None), P("dp", val)),
        check_vma=False,
    )
```

```python
import functools

import jax
import jax.numpy as jnp
from jax import lax
from jax.experimental import pallas as pl
from jax.experimental.pallas import tpu as pltpu
from jax.sharding import Mesh
from jax.sharding import PartitionSpec as P

CH = 16
HH = 64
WW = 64
ITERS = 4
LANES = 128


blur = 0.1


def sinkhorn_kernel(scale, cross_ref, noise_ref, coupled_ref):
    scores = cross_ref[...] * scale
    col = jnp.zeros((1, scores.shape[1]), jnp.float32)
    for step in range(ITERS):
        shifted = scores + col
        top = jnp.max(shifted, axis=1, keepdims=True)
        total = jnp.sum(jnp.exp(shifted - top), axis=1, keepdims=True)
        row = -(top + jnp.log(total))
        shifted = scores + row
        top = jnp.max(shifted, axis=0, keepdims=True)
        total = jnp.sum(jnp.exp(shifted - top), axis=0, keepdims=True)
        col = -(top + jnp.log(total))
    shifted = scores + col
    top = jnp.max(shifted, axis=1, keepdims=True)
    grown = jnp.exp(shifted - top)
    weights = (grown / jnp.sum(grown, axis=1, keepdims=True)).astype(jnp.bfloat16)
    coupled_ref[...] = jnp.dot(weights, noise_ref[...], preferred_element_type=jnp.float32)


def patch_rows(moved):
    chans, rows, wide = moved.shape
    strips = wide // LANES
    per = LANES // 4
    to = lax.broadcasted_iota(jnp.int32, (LANES, LANES), 0)
    come = lax.broadcasted_iota(jnp.int32, (LANES, LANES), 1)
    order = (come == to // (2 * per) * (2 * per) + to % per * 2 + to // per % 2).astype(jnp.bfloat16)
    flat = moved.reshape(chans * rows, wide)
    strip = []
    for p in range(strips):
        t = lax.dot_general(order, flat[:, p * LANES:(p + 1) * LANES], (((1,), (1,)), ((), ())),
                            preferred_element_type=jnp.float32).astype(jnp.bfloat16)
        strip.append(jnp.concatenate([t[f * per:(f + 1) * per] for f in range(4)], axis=1))
    strip = jnp.concatenate(strip, axis=0)
    k = strip.shape[1]
    come = lax.broadcasted_iota(jnp.int32, (k, k), 0)
    to = lax.broadcasted_iota(jnp.int32, (k, k), 1)
    f, c, r = come // (chans * rows), come // rows % chans, come % rows
    place = (to == r * (4 * chans) + c * 4 + f).astype(jnp.bfloat16)
    return jnp.dot(strip, place, preferred_element_type=jnp.float32).astype(jnp.bfloat16)

def embed_kernel(moved_ref, wp_ref, bias_ref, gain_ref, normed, mark_ref):
    chans, rows, wide = moved_ref.shape
    tok = wide // 4
    feat = 4 * chans
    x = patch_rows(moved_ref[...])
    for r in range(rows):
        embed = jnp.dot(x[:, r * feat:(r + 1) * feat], wp_ref[...], preferred_element_type=jnp.float32) + bias_ref[...][None, :]
        center = embed - jnp.mean(embed, axis=1, keepdims=True)
        spread = jnp.mean(center * center, axis=1, keepdims=True)
        normed[r * tok:(r + 1) * tok, :] = (center * lax.rsqrt(spread + 1e-05) * gain_ref[...][None, :]).astype(jnp.bfloat16)
    mark_ref[...] = jnp.zeros_like(mark_ref)


def a_kernel(tn, tm, side_ref, normed, w_hbm, qkv_hbm, w_buf, out_buf, w_sem, out_sem):
    tiles = w_hbm.shape[1] // tn
    ins = [
        pltpu.make_async_copy(w_hbm.at[:, pl.ds(t * tn, tn)], w_buf.at[t], w_sem.at[t])
        for t in range(tiles)
    ]
    for copy in ins:
        copy.start()
    first = side_ref[0] * tiles
    matmul(tn, tm, first, lambda t: w_buf.at[t], ins, normed, out_buf, qkv_hbm, out_sem)


def matmul(tn, tm, first, w_tile, ins, normed, out_buf, qkv_hbm, out_sem):
    n_tok = normed.shape[0]
    tiles = out_buf.shape[0]
    outs = []
    for t in range(tiles):
        if ins:
            ins[t].wait()
        w = w_tile(t)
        for m in range(0, n_tok, tm):
            out_buf[t, m:m + tm, :] = jnp.dot(
                normed[m:m + tm, :], w[...], preferred_element_type=jnp.float32
            ).astype(jnp.bfloat16)
        col = pl.multiple_of((first + t) * tn, tn)
        copy = pltpu.make_async_copy(out_buf.at[t], qkv_hbm.at[:, pl.ds(col, tn)], out_sem.at[t])
        copy.start()
        outs.append(copy)
    for copy in outs:
        copy.wait()


def b_kernel(tn, tm, side_ref, normed, w_ref, old, qkv_hbm, out_buf, out_sem):
    tiles = out_buf.shape[0]
    first = (1 - side_ref[0]) * tiles
    matmul(tn, tm, first, lambda t: w_ref.at[:, t * tn:(t + 1) * tn], None, normed, out_buf, qkv_hbm, out_sem)


def embed_tokens(moved, w_patch, bias, gain):
    vm = pl.BlockSpec(memory_space=pltpu.VMEM)
    n_tok = moved.size // w_patch.shape[0]
    return pl.pallas_call(
        embed_kernel,
        in_specs=[vm] * 4,
        out_specs=[vm, vm],
        out_shape=[
            jax.ShapeDtypeStruct((n_tok, w_patch.shape[1]), jnp.bfloat16),
            jax.ShapeDtypeStruct((8, LANES), jnp.float32),
        ],
        compiler_params=pltpu.CompilerParams(vmem_limit_bytes=32 * 2**20),
    )(moved, w_patch, bias, gain)


def first_half(side, normed, w_half, tn, tm):
    n_tok, hid = normed.shape
    half = w_half.shape[1]
    tiles = half // tn
    vm = pl.BlockSpec(memory_space=pltpu.VMEM)
    anym = pl.BlockSpec(memory_space=pl.ANY)
    return pl.pallas_call(
        functools.partial(a_kernel, tn, tm),
        in_specs=[pl.BlockSpec(memory_space=pltpu.SMEM), vm, anym],
        out_specs=anym,
        out_shape=jax.ShapeDtypeStruct((n_tok, 2 * half), jnp.bfloat16),
        scratch_shapes=[
            pltpu.VMEM((tiles, hid, tn), jnp.bfloat16),
            pltpu.VMEM((tiles, n_tok, tn), jnp.bfloat16),
            pltpu.SemaphoreType.DMA((tiles,)),
            pltpu.SemaphoreType.DMA((tiles,)),
        ],
        compiler_params=pltpu.CompilerParams(vmem_limit_bytes=48 * 2**20),
        cost_estimate=pl.CostEstimate(flops=2 * n_tok * hid * half, bytes_accessed=2 * hid * half, transcendentals=0),
    )(side, normed, w_half)


def second_half(side, normed, w_half, qkv, tn, tm):
    n_tok, hid = normed.shape
    half = w_half.shape[1]
    tiles = half // tn
    vm = pl.BlockSpec(memory_space=pltpu.VMEM)
    anym = pl.BlockSpec(memory_space=pl.ANY)
    return pl.pallas_call(
        functools.partial(b_kernel, tn, tm),
        in_specs=[pl.BlockSpec(memory_space=pltpu.SMEM), vm, vm, anym],
        out_specs=anym,
        out_shape=jax.ShapeDtypeStruct(qkv.shape, jnp.bfloat16),
        input_output_aliases={3: 0},
        scratch_shapes=[pltpu.VMEM((tiles, n_tok, tn), jnp.bfloat16), pltpu.SemaphoreType.DMA((tiles,))],
        compiler_params=pltpu.CompilerParams(vmem_limit_bytes=44 * 2**20),
        cost_estimate=pl.CostEstimate(flops=2 * n_tok * hid * half, bytes_accessed=2 * hid * half, transcendentals=0),
    )(side, normed, w_half, qkv)


def per_device(data, noise, times, w_patch, patch_bias, norm_gain, w_qkv):
    row_count, val_width = data.shape
    dp_devices = lax.axis_size("dp")
    val = ("x", "core")
    val_devices = lax.axis_size(val)
    rows = row_count * dp_devices
    part = val_width // dp_devices
    everyone = ("dp", "x", "core")
    local_chan = CH // val_devices
    strip = HH // val_devices * WW
    pieces = strip // part
    half = w_qkv.shape[1] // 2
    side = lax.axis_index("core")
    w_own = lax.dynamic_slice_in_dim(w_qkv, side * half, half, axis=1)
    w_own = lax.all_gather(w_own, "dp", axis=0, tiled=True)
    pair = jnp.concatenate([data, noise], axis=0)
    pair = jnp.transpose(pair.reshape(2 * row_count, dp_devices, part), (1, 0, 2))
    pair = lax.all_to_all(pair, "dp", split_axis=0, concat_axis=0, tiled=True)
    data_part = pair[:, :row_count].reshape(rows, part)
    noise_part = pair[:, row_count:].reshape(rows, part)
    cross = lax.dot_general(
        data_part, noise_part, (((1,), (1,)), ((), ())), preferred_element_type=jnp.float32
    )
    cross = cross.reshape(rows, rows // LANES, LANES)
    cross = lax.all_to_all(cross, everyone, split_axis=0, concat_axis=0, tiled=True)
    own = jnp.sum(cross, axis=0, keepdims=True)
    own = jnp.broadcast_to(own, (rows, rows // LANES, LANES))
    cross = lax.all_to_all(own, everyone, split_axis=0, concat_axis=0, tiled=True)
    cross = cross.reshape(rows, rows)
    scale = 1.0 / (float(val_width * val_devices) ** 0.5 * blur)
    coupled = pl.pallas_call(
        functools.partial(sinkhorn_kernel, scale),
        out_shape=jax.ShapeDtypeStruct((rows, part), jnp.float32),
        in_specs=[pl.BlockSpec(memory_space=pltpu.VMEM)] * 2,
        out_specs=pl.BlockSpec(memory_space=pltpu.VMEM),
        compiler_params=pltpu.CompilerParams(vmem_limit_bytes=16 * 2**20),
    )(cross, noise_part)
    coupled = coupled.reshape(dp_devices, row_count, part)
    coupled = lax.all_to_all(coupled, "dp", split_axis=0, concat_axis=0, tiled=True)
    own_data = jnp.transpose(data.reshape(row_count, dp_devices, part), (1, 0, 2)).astype(jnp.float32)
    blend = times[None, :, None]
    mixed = ((1.0 - blend) * coupled + blend * own_data).astype(jnp.bfloat16)
    target = (own_data - coupled).astype(jnp.bfloat16)
    target = jnp.transpose(target, (1, 0, 2)).reshape(row_count, val_width)
    mixed = mixed.reshape(local_chan, val_devices, pieces, row_count, part)
    mixed = jnp.transpose(mixed, (1, 0, 3, 2, 4)).reshape(val_devices, local_chan, row_count, strip)
    moved = lax.all_to_all(mixed, val, split_axis=0, concat_axis=0, tiled=True)
    moved = moved.reshape(CH, row_count, strip)
    side = side.astype(jnp.int32).reshape(1)
    normed, mark = embed_tokens(moved, w_patch, patch_bias, norm_gain)
    mark, w_own = lax.optimization_barrier((mark, w_own))
    w_other = lax.ppermute(w_own, "core", [(0, 1), (1, 0)])
    qkv = first_half(side, normed, w_own, 768, 256)
    qkv = second_half(side, normed, w_other, qkv, 768, 256)
    return (qkv.reshape(row_count, -1, 2 * half), target)


def solution(mesh):
    devices = mesh.devices
    fine = Mesh(devices.reshape(devices.shape[0], -1, 2), ("dp", "x", "core"))
    val = ("x", "core")
    return jax.shard_map(
        per_device,
        mesh=fine,
        in_specs=(P("dp", val), P("dp", val), P("dp"), P(), P(), P(), P("dp", None)),
        out_specs=(P("dp", val, None), P("dp", val)),
        check_vma=False,
    )
```

```python
import functools

import jax
import jax.numpy as jnp
from jax import lax
from jax.experimental import pallas as pl
from jax.experimental.pallas import tpu as pltpu
from jax.sharding import Mesh
from jax.sharding import PartitionSpec as P

CH = 16
HH = 64
WW = 64
ITERS = 4
LANES = 128


blur = 0.1


def sinkhorn_kernel(scale, cross_ref, noise_ref, coupled_ref):
    scores = cross_ref[...] * scale
    col = jnp.zeros((1, scores.shape[1]), jnp.float32)
    for step in range(ITERS):
        shifted = scores + col
        top = jnp.max(shifted, axis=1, keepdims=True)
        total = jnp.sum(jnp.exp(shifted - top), axis=1, keepdims=True)
        row = -(top + jnp.log(total))
        shifted = scores + row
        top = jnp.max(shifted, axis=0, keepdims=True)
        total = jnp.sum(jnp.exp(shifted - top), axis=0, keepdims=True)
        col = -(top + jnp.log(total))
    shifted = scores + col
    top = jnp.max(shifted, axis=1, keepdims=True)
    grown = jnp.exp(shifted - top)
    weights = (grown / jnp.sum(grown, axis=1, keepdims=True)).astype(jnp.bfloat16)
    coupled_ref[...] = jnp.dot(weights, noise_ref[...], preferred_element_type=jnp.float32)


def patch_rows(moved):
    chans, rows, wide = moved.shape
    strips = wide // LANES
    per = LANES // 4
    to = lax.broadcasted_iota(jnp.int32, (LANES, LANES), 0)
    come = lax.broadcasted_iota(jnp.int32, (LANES, LANES), 1)
    order = (come == to // (2 * per) * (2 * per) + to % per * 2 + to // per % 2).astype(jnp.bfloat16)
    flat = moved.reshape(chans * rows, wide)
    strip = []
    for p in range(strips):
        t = lax.dot_general(order, flat[:, p * LANES:(p + 1) * LANES], (((1,), (1,)), ((), ())),
                            preferred_element_type=jnp.float32).astype(jnp.bfloat16)
        strip.append(jnp.concatenate([t[f * per:(f + 1) * per] for f in range(4)], axis=1))
    strip = jnp.concatenate(strip, axis=0)
    k = strip.shape[1]
    come = lax.broadcasted_iota(jnp.int32, (k, k), 0)
    to = lax.broadcasted_iota(jnp.int32, (k, k), 1)
    f, c, r = come // (chans * rows), come // rows % chans, come % rows
    place = (to == r * (4 * chans) + c * 4 + f).astype(jnp.bfloat16)
    return jnp.dot(strip, place, preferred_element_type=jnp.float32).astype(jnp.bfloat16)

def embed_kernel(moved_ref, wp_ref, bias_ref, gain_ref, normed, mark_ref):
    chans, rows, wide = moved_ref.shape
    tok = wide // 4
    feat = 4 * chans
    x = patch_rows(moved_ref[...])
    for r in range(rows):
        embed = jnp.dot(x[:, r * feat:(r + 1) * feat], wp_ref[...], preferred_element_type=jnp.float32) + bias_ref[...][None, :]
        center = embed - jnp.mean(embed, axis=1, keepdims=True)
        spread = jnp.mean(center * center, axis=1, keepdims=True)
        normed[r * tok:(r + 1) * tok, :] = (center * lax.rsqrt(spread + 1e-05) * gain_ref[...][None, :]).astype(jnp.bfloat16)
    mark_ref[...] = jnp.zeros_like(mark_ref)


def a_kernel(tn, tm, side_ref, mark_ref, normed, w_hbm, qkv_hbm, w_buf, out_buf, w_sem, out_sem):
    tiles = w_hbm.shape[1] // tn
    ins = [
        pltpu.make_async_copy(w_hbm.at[:, pl.ds(t * tn, tn)], w_buf.at[t], w_sem.at[t])
        for t in range(tiles)
    ]
    for copy in ins:
        copy.start()
    first = side_ref[0] * tiles
    matmul(tn, tm, first, lambda t: w_buf.at[t], ins, normed, out_buf, qkv_hbm, out_sem)


def matmul(tn, tm, first, w_tile, ins, normed, out_buf, qkv_hbm, out_sem):
    n_tok = normed.shape[0]
    tiles = out_buf.shape[0]
    outs = []
    for t in range(tiles):
        if ins:
            ins[t].wait()
        w = w_tile(t)
        for m in range(0, n_tok, tm):
            out_buf[t, m:m + tm, :] = jnp.dot(
                normed[m:m + tm, :], w[...], preferred_element_type=jnp.float32
            ).astype(jnp.bfloat16)
        col = pl.multiple_of((first + t) * tn, tn)
        copy = pltpu.make_async_copy(out_buf.at[t], qkv_hbm.at[:, pl.ds(col, tn)], out_sem.at[t])
        copy.start()
        outs.append(copy)
    for copy in outs:
        copy.wait()


def b_kernel(tn, tm, side_ref, normed, w_ref, old, qkv_hbm, out_buf, out_sem):
    tiles = out_buf.shape[0]
    first = (1 - side_ref[0]) * tiles
    matmul(tn, tm, first, lambda t: w_ref.at[:, t * tn:(t + 1) * tn], None, normed, out_buf, qkv_hbm, out_sem)


def embed_tokens(moved, w_patch, bias, gain):
    vm = pl.BlockSpec(memory_space=pltpu.VMEM)
    n_tok = moved.size // w_patch.shape[0]
    return pl.pallas_call(
        embed_kernel,
        in_specs=[vm] * 4,
        out_specs=[vm, vm],
        out_shape=[
            jax.ShapeDtypeStruct((n_tok, w_patch.shape[1]), jnp.bfloat16),
            jax.ShapeDtypeStruct((8, LANES), jnp.float32),
        ],
        compiler_params=pltpu.CompilerParams(vmem_limit_bytes=24 * 2**20),
    )(moved, w_patch, bias, gain)


def first_half(side, mark, normed, w_half, tn, tm):
    n_tok, hid = normed.shape
    half = w_half.shape[1]
    tiles = half // tn
    vm = pl.BlockSpec(memory_space=pltpu.VMEM)
    hbm = pl.BlockSpec(memory_space=pltpu.HBM)
    return pl.pallas_call(
        functools.partial(a_kernel, tn, tm),
        in_specs=[pl.BlockSpec(memory_space=pltpu.SMEM), vm, vm, hbm],
        out_specs=hbm,
        out_shape=jax.ShapeDtypeStruct((n_tok, 2 * half), jnp.bfloat16),
        scratch_shapes=[
            pltpu.VMEM((tiles, hid, tn), jnp.bfloat16),
            pltpu.VMEM((tiles, n_tok, tn), jnp.bfloat16),
            pltpu.SemaphoreType.DMA((tiles,)),
            pltpu.SemaphoreType.DMA((tiles,)),
        ],
        compiler_params=pltpu.CompilerParams(vmem_limit_bytes=48 * 2**20),
        cost_estimate=pl.CostEstimate(flops=2 * n_tok * hid * half, bytes_accessed=2 * hid * half, transcendentals=0),
    )(side, mark, normed, w_half)


def second_half(side, normed, w_half, qkv, tn, tm):
    n_tok, hid = normed.shape
    half = w_half.shape[1]
    tiles = half // tn
    vm = pl.BlockSpec(memory_space=pltpu.VMEM)
    hbm = pl.BlockSpec(memory_space=pltpu.HBM)
    return pl.pallas_call(
        functools.partial(b_kernel, tn, tm),
        in_specs=[pl.BlockSpec(memory_space=pltpu.SMEM), vm, vm, hbm],
        out_specs=hbm,
        out_shape=jax.ShapeDtypeStruct(qkv.shape, jnp.bfloat16),
        input_output_aliases={3: 0},
        scratch_shapes=[pltpu.VMEM((tiles, n_tok, tn), jnp.bfloat16), pltpu.SemaphoreType.DMA((tiles,))],
        compiler_params=pltpu.CompilerParams(vmem_limit_bytes=20 * 2**20),
        cost_estimate=pl.CostEstimate(flops=2 * n_tok * hid * half, bytes_accessed=2 * hid * half, transcendentals=0),
    )(side, normed, w_half, qkv)


def per_device(data, noise, times, w_patch, patch_bias, norm_gain, w_qkv):
    row_count, val_width = data.shape
    dp_devices = lax.axis_size("dp")
    val = ("x", "core")
    val_devices = lax.axis_size(val)
    rows = row_count * dp_devices
    part = val_width // dp_devices
    everyone = ("dp", "x", "core")
    local_chan = CH // val_devices
    strip = HH // val_devices * WW
    pieces = strip // part
    half = w_qkv.shape[1] // 2
    side = lax.axis_index("core")
    w_own = lax.dynamic_slice_in_dim(w_qkv, side * half, half, axis=1)
    w_own = lax.all_gather(w_own, "dp", axis=0, tiled=True)
    pair = jnp.concatenate([data, noise], axis=0)
    pair = jnp.transpose(pair.reshape(2 * row_count, dp_devices, part), (1, 0, 2))
    pair = lax.all_to_all(pair, "dp", split_axis=0, concat_axis=0, tiled=True)
    data_part = pair[:, :row_count].reshape(rows, part)
    noise_part = pair[:, row_count:].reshape(rows, part)
    cross = lax.dot_general(
        data_part, noise_part, (((1,), (1,)), ((), ())), preferred_element_type=jnp.float32
    )
    cross = cross.reshape(rows, rows // LANES, LANES)
    cross = lax.all_to_all(cross, everyone, split_axis=0, concat_axis=0, tiled=True)
    own = jnp.sum(cross, axis=0, keepdims=True)
    own = jnp.broadcast_to(own, (rows, rows // LANES, LANES))
    cross = lax.all_to_all(own, everyone, split_axis=0, concat_axis=0, tiled=True)
    cross = cross.reshape(rows, rows)
    scale = 1.0 / (float(val_width * val_devices) ** 0.5 * blur)
    coupled = pl.pallas_call(
        functools.partial(sinkhorn_kernel, scale),
        out_shape=jax.ShapeDtypeStruct((rows, part), jnp.float32),
        in_specs=[pl.BlockSpec(memory_space=pltpu.VMEM)] * 2,
        out_specs=pl.BlockSpec(memory_space=pltpu.VMEM),
        compiler_params=pltpu.CompilerParams(vmem_limit_bytes=16 * 2**20),
    )(cross, noise_part)
    coupled = coupled.reshape(dp_devices, row_count, part)
    coupled = lax.all_to_all(coupled, "dp", split_axis=0, concat_axis=0, tiled=True)
    own_data = jnp.transpose(data.reshape(row_count, dp_devices, part), (1, 0, 2)).astype(jnp.float32)
    blend = times[None, :, None]
    mixed = ((1.0 - blend) * coupled + blend * own_data).astype(jnp.bfloat16)
    target = (own_data - coupled).astype(jnp.bfloat16)
    target = jnp.transpose(target, (1, 0, 2)).reshape(row_count, val_width)
    mixed = mixed.reshape(local_chan, val_devices, pieces, row_count, part)
    mixed = jnp.transpose(mixed, (1, 0, 3, 2, 4)).reshape(val_devices, local_chan, row_count, strip)
    moved = lax.all_to_all(mixed, val, split_axis=0, concat_axis=0, tiled=True)
    moved = moved.reshape(CH, row_count, strip)
    side = side.astype(jnp.int32).reshape(1)
    normed, mark = embed_tokens(moved, w_patch, patch_bias, norm_gain)
    mark, w_own = lax.optimization_barrier((mark, w_own))
    w_other = lax.ppermute(w_own, "core", [(0, 1), (1, 0)])
    qkv = first_half(side, mark, normed, w_own, 768, 256)
    qkv = second_half(side, normed, w_other, qkv, 768, 256)
    return (qkv.reshape(row_count, -1, 2 * half), target)


def solution(mesh):
    devices = mesh.devices
    fine = Mesh(devices.reshape(devices.shape[0], -1, 2), ("dp", "x", "core"))
    val = ("x", "core")
    return jax.shard_map(
        per_device,
        mesh=fine,
        in_specs=(P("dp", val), P("dp", val), P("dp"), P(), P(), P(), P("dp", None)),
        out_specs=(P("dp", val, None), P("dp", val)),
        check_vma=False,
    )
```

```python
import functools

import jax
import jax.numpy as jnp
from jax import lax
from jax.experimental import pallas as pl
from jax.experimental.pallas import tpu as pltpu
from jax.sharding import Mesh
from jax.sharding import PartitionSpec as P

CH = 16
HH = 64
WW = 64
ITERS = 4
LANES = 128


blur = 0.1


def sinkhorn_kernel(scale, cross_ref, noise_ref, coupled_ref):
    scores = cross_ref[...] * scale
    col = jnp.zeros((1, scores.shape[1]), jnp.float32)
    for step in range(ITERS):
        shifted = scores + col
        top = jnp.max(shifted, axis=1, keepdims=True)
        total = jnp.sum(jnp.exp(shifted - top), axis=1, keepdims=True)
        row = -(top + jnp.log(total))
        shifted = scores + row
        top = jnp.max(shifted, axis=0, keepdims=True)
        total = jnp.sum(jnp.exp(shifted - top), axis=0, keepdims=True)
        col = -(top + jnp.log(total))
    shifted = scores + col
    top = jnp.max(shifted, axis=1, keepdims=True)
    grown = jnp.exp(shifted - top)
    weights = (grown / jnp.sum(grown, axis=1, keepdims=True)).astype(jnp.bfloat16)
    coupled_ref[...] = jnp.dot(weights, noise_ref[...], preferred_element_type=jnp.float32)


def patch_rows(moved):
    chans, rows, wide = moved.shape
    strips = wide // LANES
    per = LANES // 4
    to = lax.broadcasted_iota(jnp.int32, (LANES, LANES), 0)
    come = lax.broadcasted_iota(jnp.int32, (LANES, LANES), 1)
    order = (come == to // (2 * per) * (2 * per) + to % per * 2 + to // per % 2).astype(jnp.bfloat16)
    flat = moved.reshape(chans * rows, wide)
    strip = []
    for p in range(strips):
        t = lax.dot_general(order, flat[:, p * LANES:(p + 1) * LANES], (((1,), (1,)), ((), ())),
                            preferred_element_type=jnp.float32).astype(jnp.bfloat16)
        strip.append(jnp.concatenate([t[f * per:(f + 1) * per] for f in range(4)], axis=1))
    strip = jnp.concatenate(strip, axis=0)
    k = strip.shape[1]
    come = lax.broadcasted_iota(jnp.int32, (k, k), 0)
    to = lax.broadcasted_iota(jnp.int32, (k, k), 1)
    f, c, r = come // (chans * rows), come // rows % chans, come % rows
    place = (to == r * (4 * chans) + c * 4 + f).astype(jnp.bfloat16)
    return jnp.dot(strip, place, preferred_element_type=jnp.float32).astype(jnp.bfloat16)

def embed_kernel(moved_ref, wp_ref, bias_ref, gain_ref, normed, mark_ref):
    chans, rows, wide = moved_ref.shape
    tok = wide // 4
    feat = 4 * chans
    x = patch_rows(moved_ref[...])
    for r in range(rows):
        embed = jnp.dot(x[:, r * feat:(r + 1) * feat], wp_ref[...], preferred_element_type=jnp.float32) + bias_ref[...][None, :]
        center = embed - jnp.mean(embed, axis=1, keepdims=True)
        spread = jnp.mean(center * center, axis=1, keepdims=True)
        normed[r * tok:(r + 1) * tok, :] = (center * lax.rsqrt(spread + 1e-05) * gain_ref[...][None, :]).astype(jnp.bfloat16)
    mark_ref[...] = jnp.zeros_like(mark_ref)


def spans(widths):
    ends = [sum(widths[:t + 1]) for t in range(len(widths))]
    return [(end - width, end) for end, width in zip(ends, widths)]


def a_kernel(cols, tm, side_ref, mark_ref, normed, w_hbm, qkv_hbm, w_buf, out_buf, w_sem, out_sem):
    ins = [
        pltpu.make_async_copy(w_hbm.at[:, a:b], w_buf.at[:, a:b], w_sem.at[t])
        for t, (a, b) in enumerate(cols)
    ]
    for copy in ins:
        copy.start()
    first = side_ref[0] * w_hbm.shape[1]
    matmul(cols, tm, first, w_buf, ins, normed, out_buf, qkv_hbm, out_sem)


def matmul(cols, tm, first, w_ref, ins, normed, out_buf, qkv_hbm, out_sem):
    n_tok = normed.shape[0]
    outs = []
    for t, (a, b) in enumerate(cols):
        if ins:
            ins[t].wait()
        for m in range(0, n_tok, tm):
            out_buf[m:m + tm, a:b] = jnp.dot(
                normed[m:m + tm, :], w_ref[:, a:b], preferred_element_type=jnp.float32
            ).astype(jnp.bfloat16)
        at = pl.multiple_of(first + a, 2 * LANES)
        copy = pltpu.make_async_copy(out_buf.at[:, a:b], qkv_hbm.at[:, pl.ds(at, b - a)], out_sem.at[t])
        copy.start()
        outs.append(copy)
    for copy in outs:
        copy.wait()


def b_kernel(cols, tm, side_ref, normed, w_ref, old, qkv_hbm, out_buf, out_sem):
    first = (1 - side_ref[0]) * w_ref.shape[1]
    matmul(cols, tm, first, w_ref, None, normed, out_buf, qkv_hbm, out_sem)


def embed_tokens(moved, w_patch, bias, gain):
    vm = pl.BlockSpec(memory_space=pltpu.VMEM)
    n_tok = moved.size // w_patch.shape[0]
    return pl.pallas_call(
        embed_kernel,
        in_specs=[vm] * 4,
        out_specs=[vm, vm],
        out_shape=[
            jax.ShapeDtypeStruct((n_tok, w_patch.shape[1]), jnp.bfloat16),
            jax.ShapeDtypeStruct((8, LANES), jnp.float32),
        ],
        compiler_params=pltpu.CompilerParams(vmem_limit_bytes=48 * 2**20),
    )(moved, w_patch, bias, gain)


def first_half(side, mark, normed, w_half, widths, tm):
    n_tok, hid = normed.shape
    half = w_half.shape[1]
    cols = spans(widths)
    vm = pl.BlockSpec(memory_space=pltpu.VMEM)
    hbm = pl.BlockSpec(memory_space=pltpu.HBM)
    return pl.pallas_call(
        functools.partial(a_kernel, cols, tm),
        in_specs=[pl.BlockSpec(memory_space=pltpu.SMEM), vm, vm, hbm],
        out_specs=hbm,
        out_shape=jax.ShapeDtypeStruct((n_tok, 2 * half), jnp.bfloat16),
        scratch_shapes=[
            pltpu.VMEM((hid, half), jnp.bfloat16),
            pltpu.VMEM((n_tok, half), jnp.bfloat16),
            pltpu.SemaphoreType.DMA((len(cols),)),
            pltpu.SemaphoreType.DMA((len(cols),)),
        ],
        compiler_params=pltpu.CompilerParams(vmem_limit_bytes=48 * 2**20),
        cost_estimate=pl.CostEstimate(flops=2 * n_tok * hid * half, bytes_accessed=2 * hid * half, transcendentals=0),
    )(side, mark, normed, w_half)


def second_half(side, normed, w_half, qkv, widths, tm):
    n_tok, hid = normed.shape
    half = w_half.shape[1]
    cols = spans(widths)
    vm = pl.BlockSpec(memory_space=pltpu.VMEM)
    hbm = pl.BlockSpec(memory_space=pltpu.HBM)
    return pl.pallas_call(
        functools.partial(b_kernel, cols, tm),
        in_specs=[pl.BlockSpec(memory_space=pltpu.SMEM), vm, vm, hbm],
        out_specs=hbm,
        out_shape=jax.ShapeDtypeStruct(qkv.shape, jnp.bfloat16),
        input_output_aliases={3: 0},
        scratch_shapes=[pltpu.VMEM((n_tok, half), jnp.bfloat16), pltpu.SemaphoreType.DMA((len(cols),))],
        compiler_params=pltpu.CompilerParams(vmem_limit_bytes=20 * 2**20),
        cost_estimate=pl.CostEstimate(flops=2 * n_tok * hid * half, bytes_accessed=2 * hid * half, transcendentals=0),
    )(side, normed, w_half, qkv)


def per_device(data, noise, times, w_patch, patch_bias, norm_gain, w_qkv):
    row_count, val_width = data.shape
    dp_devices = lax.axis_size("dp")
    val = ("x", "core")
    val_devices = lax.axis_size(val)
    rows = row_count * dp_devices
    part = val_width // dp_devices
    everyone = ("dp", "x", "core")
    local_chan = CH // val_devices
    strip = HH // val_devices * WW
    pieces = strip // part
    half = w_qkv.shape[1] // 2
    side = lax.axis_index("core")
    w_own = lax.dynamic_slice_in_dim(w_qkv, side * half, half, axis=1)
    w_own = lax.all_gather(w_own, "dp", axis=0, tiled=True)
    pair = jnp.concatenate([data, noise], axis=0)
    pair = jnp.transpose(pair.reshape(2 * row_count, dp_devices, part), (1, 0, 2))
    pair = lax.all_to_all(pair, "dp", split_axis=0, concat_axis=0, tiled=True)
    data_part = pair[:, :row_count].reshape(rows, part)
    noise_part = pair[:, row_count:].reshape(rows, part)
    cross = lax.dot_general(
        data_part, noise_part, (((1,), (1,)), ((), ())), preferred_element_type=jnp.float32
    )
    cross = cross.reshape(rows, rows // LANES, LANES)
    cross = lax.all_to_all(cross, everyone, split_axis=0, concat_axis=0, tiled=True)
    own = jnp.sum(cross, axis=0, keepdims=True)
    own = jnp.broadcast_to(own, (rows, rows // LANES, LANES))
    cross = lax.all_to_all(own, everyone, split_axis=0, concat_axis=0, tiled=True)
    cross = cross.reshape(rows, rows)
    scale = 1.0 / (float(val_width * val_devices) ** 0.5 * blur)
    coupled = pl.pallas_call(
        functools.partial(sinkhorn_kernel, scale),
        out_shape=jax.ShapeDtypeStruct((rows, part), jnp.float32),
        in_specs=[pl.BlockSpec(memory_space=pltpu.VMEM)] * 2,
        out_specs=pl.BlockSpec(memory_space=pltpu.VMEM),
        compiler_params=pltpu.CompilerParams(vmem_limit_bytes=16 * 2**20),
    )(cross, noise_part)
    coupled = coupled.reshape(dp_devices, row_count, part)
    coupled = lax.all_to_all(coupled, "dp", split_axis=0, concat_axis=0, tiled=True)
    own_data = jnp.transpose(data.reshape(row_count, dp_devices, part), (1, 0, 2)).astype(jnp.float32)
    blend = times[None, :, None]
    mixed = ((1.0 - blend) * coupled + blend * own_data).astype(jnp.bfloat16)
    target = (own_data - coupled).astype(jnp.bfloat16)
    target = jnp.transpose(target, (1, 0, 2)).reshape(row_count, val_width)
    mixed = mixed.reshape(local_chan, val_devices, pieces, row_count, part)
    mixed = jnp.transpose(mixed, (1, 0, 3, 2, 4)).reshape(val_devices, local_chan, row_count, strip)
    moved = lax.all_to_all(mixed, val, split_axis=0, concat_axis=0, tiled=True)
    moved = moved.reshape(CH, row_count, strip)
    side = side.astype(jnp.int32).reshape(1)
    normed, mark = embed_tokens(moved, w_patch, patch_bias, norm_gain)
    mark, w_own = lax.optimization_barrier((mark, w_own))
    w_other = lax.ppermute(w_own, "core", [(0, 1), (1, 0)])
    qkv = first_half(side, mark, normed, w_own, (256, 512, 768, 512, 256), 256)
    qkv = second_half(side, normed, w_other, qkv, (768, 768, 512, 256), 256)
    return (qkv.reshape(row_count, -1, 2 * half), target)


def solution(mesh):
    devices = mesh.devices
    fine = Mesh(devices.reshape(devices.shape[0], -1, 2), ("dp", "x", "core"))
    val = ("x", "core")
    return jax.shard_map(
        per_device,
        mesh=fine,
        in_specs=(P("dp", val), P("dp", val), P("dp"), P(), P(), P(), P("dp", None)),
        out_specs=(P("dp", val, None), P("dp", val)),
        check_vma=False,
    )
```

```python
import functools

import jax
import jax.numpy as jnp
from jax import lax
from jax.experimental import pallas as pl
from jax.experimental.pallas import tpu as pltpu
from jax.sharding import Mesh
from jax.sharding import PartitionSpec as P

CH = 16
HH = 64
WW = 64
ITERS = 4
LANES = 128


blur = 0.1


def sinkhorn_kernel(scale, cross_ref, noise_ref, coupled_ref):
    scores = cross_ref[...] * scale
    col = jnp.zeros((1, scores.shape[1]), jnp.float32)
    for step in range(ITERS):
        shifted = scores + col
        top = jnp.max(shifted, axis=1, keepdims=True)
        total = jnp.sum(jnp.exp(shifted - top), axis=1, keepdims=True)
        row = -(top + jnp.log(total))
        shifted = scores + row
        top = jnp.max(shifted, axis=0, keepdims=True)
        total = jnp.sum(jnp.exp(shifted - top), axis=0, keepdims=True)
        col = -(top + jnp.log(total))
    shifted = scores + col
    top = jnp.max(shifted, axis=1, keepdims=True)
    grown = jnp.exp(shifted - top)
    weights = (grown / jnp.sum(grown, axis=1, keepdims=True)).astype(jnp.bfloat16)
    coupled_ref[...] = jnp.dot(weights, noise_ref[...], preferred_element_type=jnp.float32)


def patch_rows(moved):
    chans, rows, wide = moved.shape
    strips = wide // LANES
    per = LANES // 4
    to = lax.broadcasted_iota(jnp.int32, (LANES, LANES), 0)
    come = lax.broadcasted_iota(jnp.int32, (LANES, LANES), 1)
    order = (come == to // (2 * per) * (2 * per) + to % per * 2 + to // per % 2).astype(jnp.bfloat16)
    flat = moved.reshape(chans * rows, wide)
    strip = []
    for p in range(strips):
        t = lax.dot_general(order, flat[:, p * LANES:(p + 1) * LANES], (((1,), (1,)), ((), ())),
                            preferred_element_type=jnp.float32).astype(jnp.bfloat16)
        strip.append(jnp.concatenate([t[f * per:(f + 1) * per] for f in range(4)], axis=1))
    strip = jnp.concatenate(strip, axis=0)
    k = strip.shape[1]
    come = lax.broadcasted_iota(jnp.int32, (k, k), 0)
    to = lax.broadcasted_iota(jnp.int32, (k, k), 1)
    f, c, r = come // (chans * rows), come // rows % chans, come % rows
    place = (to == r * (4 * chans) + c * 4 + f).astype(jnp.bfloat16)
    return jnp.dot(strip, place, preferred_element_type=jnp.float32).astype(jnp.bfloat16)

def mix_kernel(times_ref, coupled_ref, data_ref, target_ref, mixed_ref):
    count, rows, part = coupled_ref.shape
    blocks, chans, _, strip = mixed_ref.shape
    pieces = strip // part
    row = lax.broadcasted_iota(jnp.int32, (rows, part), 0)
    blend = jnp.zeros((rows, part), jnp.float32)
    for r in range(rows):
        blend = jnp.where(row == r, times_ref[r], blend)
    for k in range(count):
        chan, block, piece = k // (blocks * pieces), k // pieces % blocks, k % pieces
        coupled = coupled_ref[k]
        own = data_ref[:, k * part:(k + 1) * part].astype(jnp.float32)
        target_ref[:, k * part:(k + 1) * part] = (own - coupled).astype(jnp.bfloat16)
        mixed = (1.0 - blend) * coupled + blend * own
        mixed_ref[block, chan, :, piece * part:(piece + 1) * part] = mixed.astype(jnp.bfloat16)


def embed_kernel(moved_ref, wp_ref, bias_ref, gain_ref, normed_hbm, normed, sem):
    chans, rows, wide = moved_ref.shape
    tok = wide // 4
    feat = 4 * chans
    x = patch_rows(moved_ref[...])
    copies = []
    for r in range(rows):
        embed = jnp.dot(x[:, r * feat:(r + 1) * feat], wp_ref[...], preferred_element_type=jnp.float32) + bias_ref[...][None, :]
        center = embed - jnp.mean(embed, axis=1, keepdims=True)
        spread = jnp.mean(center * center, axis=1, keepdims=True)
        at = slice(r * tok, (r + 1) * tok)
        normed[at, :] = (center * lax.rsqrt(spread + 1e-05) * gain_ref[...][None, :]).astype(jnp.bfloat16)
        copy = pltpu.make_async_copy(normed.at[at, :], normed_hbm.at[at, :], sem.at[r])
        copy.start()
        copies.append(copy)
    for copy in copies:
        copy.wait()


def spans(widths):
    ends = [sum(widths[:t + 1]) for t in range(len(widths))]
    return [(end - width, end) for end, width in zip(ends, widths)]


def a_kernel(cols, tm, side_ref, normed_hbm, w_hbm, qkv_hbm, normed, w_buf, out_buf, w_sem, n_sem, out_sem):
    n_tok = normed.shape[0]
    ins = [
        pltpu.make_async_copy(w_hbm.at[:, a:b], w_buf.at[:, a:b], w_sem.at[t])
        for t, (a, b) in enumerate(cols)
    ]
    rows = [
        pltpu.make_async_copy(normed_hbm.at[m:m + tm, :], normed.at[m:m + tm, :], n_sem.at[m // tm])
        for m in range(0, n_tok, tm)
    ]
    for copy in ins[:1] + rows + ins[1:]:
        copy.start()
    first = side_ref[0] * w_hbm.shape[1]
    matmul(cols, tm, first, w_buf, ins, rows, normed, out_buf, qkv_hbm, out_sem)


def matmul(cols, tm, first, w_ref, ins, rows, normed, out_buf, qkv_hbm, out_sem):
    n_tok = normed.shape[0]
    outs = []
    for t, (a, b) in enumerate(cols):
        if ins:
            ins[t].wait()
        for m in range(0, n_tok, tm):
            if rows and t == 0:
                rows[m // tm].wait()
            out_buf[m:m + tm, a:b] = jnp.dot(
                normed[m:m + tm, :], w_ref[:, a:b], preferred_element_type=jnp.float32
            ).astype(jnp.bfloat16)
        at = pl.multiple_of(first + a, 2 * LANES)
        copy = pltpu.make_async_copy(out_buf.at[:, a:b], qkv_hbm.at[:, pl.ds(at, b - a)], out_sem.at[t])
        copy.start()
        outs.append(copy)
    for copy in outs:
        copy.wait()


def b_kernel(cols, tm, side_ref, normed, w_ref, old, qkv_hbm, out_buf, out_sem):
    first = (1 - side_ref[0]) * w_ref.shape[1]
    matmul(cols, tm, first, w_ref, None, None, normed, out_buf, qkv_hbm, out_sem)


def mix(times, coupled, data, blocks):
    count, rows, part = coupled.shape
    vm = pl.BlockSpec(memory_space=pltpu.VMEM)
    mixed = (blocks, CH // blocks, rows, HH // blocks * WW)
    return pl.pallas_call(
        mix_kernel,
        in_specs=[pl.BlockSpec(memory_space=pltpu.SMEM), vm, vm],
        out_specs=[vm, vm],
        out_shape=[jax.ShapeDtypeStruct(data.shape, jnp.bfloat16), jax.ShapeDtypeStruct(mixed, jnp.bfloat16)],
    )(times, coupled, data)


def embed_tokens(moved, w_patch, bias, gain):
    chans, rows, wide = moved.shape
    vm = pl.BlockSpec(memory_space=pltpu.VMEM)
    shape = (moved.size // w_patch.shape[0], w_patch.shape[1])
    return pl.pallas_call(
        embed_kernel,
        in_specs=[vm] * 4,
        out_specs=pl.BlockSpec(memory_space=pltpu.HBM),
        out_shape=jax.ShapeDtypeStruct(shape, jnp.bfloat16),
        scratch_shapes=[pltpu.VMEM(shape, jnp.bfloat16), pltpu.SemaphoreType.DMA((rows,))],
        compiler_params=pltpu.CompilerParams(vmem_limit_bytes=58 * 2**20),
    )(moved, w_patch, bias, gain)


def first_half(side, normed, w_half, widths, tm):
    n_tok, hid = normed.shape
    half = w_half.shape[1]
    cols = spans(widths)
    vm = pl.BlockSpec(memory_space=pltpu.VMEM)
    hbm = pl.BlockSpec(memory_space=pltpu.HBM)
    return pl.pallas_call(
        functools.partial(a_kernel, cols, tm),
        in_specs=[pl.BlockSpec(memory_space=pltpu.SMEM), hbm, hbm],
        out_specs=[hbm, vm],
        out_shape=[
            jax.ShapeDtypeStruct((n_tok, 2 * half), jnp.bfloat16),
            jax.ShapeDtypeStruct((n_tok, hid), jnp.bfloat16),
        ],
        scratch_shapes=[
            pltpu.VMEM((hid, half), jnp.bfloat16),
            pltpu.VMEM((n_tok, half), jnp.bfloat16),
            pltpu.SemaphoreType.DMA((len(cols),)),
            pltpu.SemaphoreType.DMA((n_tok // tm,)),
            pltpu.SemaphoreType.DMA((len(cols),)),
        ],
        compiler_params=pltpu.CompilerParams(vmem_limit_bytes=48 * 2**20),
        cost_estimate=pl.CostEstimate(flops=2 * n_tok * hid * half, bytes_accessed=2 * hid * half, transcendentals=0),
    )(side, normed, w_half)


def second_half(side, normed, w_half, qkv, widths, tm):
    n_tok, hid = normed.shape
    half = w_half.shape[1]
    cols = spans(widths)
    vm = pl.BlockSpec(memory_space=pltpu.VMEM)
    hbm = pl.BlockSpec(memory_space=pltpu.HBM)
    return pl.pallas_call(
        functools.partial(b_kernel, cols, tm),
        in_specs=[pl.BlockSpec(memory_space=pltpu.SMEM), vm, vm, hbm],
        out_specs=hbm,
        out_shape=jax.ShapeDtypeStruct(qkv.shape, jnp.bfloat16),
        input_output_aliases={3: 0},
        scratch_shapes=[pltpu.VMEM((n_tok, half), jnp.bfloat16), pltpu.SemaphoreType.DMA((len(cols),))],
        compiler_params=pltpu.CompilerParams(vmem_limit_bytes=20 * 2**20),
        cost_estimate=pl.CostEstimate(flops=2 * n_tok * hid * half, bytes_accessed=2 * hid * half, transcendentals=0),
    )(side, normed, w_half, qkv)


def per_device(data, noise, times, w_patch, patch_bias, norm_gain, w_qkv):
    row_count, val_width = data.shape
    dp_devices = lax.axis_size("dp")
    val = ("x", "core")
    val_devices = lax.axis_size(val)
    rows = row_count * dp_devices
    part = val_width // dp_devices
    everyone = ("dp", "x", "core")
    local_chan = CH // val_devices
    strip = HH // val_devices * WW
    pieces = strip // part
    half = w_qkv.shape[1] // 2
    side = lax.axis_index("core")
    w_own = lax.dynamic_slice_in_dim(w_qkv, side * half, half, axis=1)
    w_own = lax.all_gather(w_own, "dp", axis=0, tiled=True)
    pair = jnp.concatenate([data, noise], axis=0)
    pair = jnp.transpose(pair.reshape(2 * row_count, dp_devices, part), (1, 0, 2))
    pair = lax.all_to_all(pair, "dp", split_axis=0, concat_axis=0, tiled=True)
    data_part = pair[:, :row_count].reshape(rows, part)
    noise_part = pair[:, row_count:].reshape(rows, part)
    cross = lax.dot_general(
        data_part, noise_part, (((1,), (1,)), ((), ())), preferred_element_type=jnp.float32
    )
    cross = cross.reshape(rows, rows // LANES, LANES)
    cross = lax.all_to_all(cross, everyone, split_axis=0, concat_axis=0, tiled=True)
    own = jnp.sum(cross, axis=0, keepdims=True)
    own = jnp.broadcast_to(own, (rows, rows // LANES, LANES))
    cross = lax.all_to_all(own, everyone, split_axis=0, concat_axis=0, tiled=True)
    cross = cross.reshape(rows, rows)
    scale = 1.0 / (float(val_width * val_devices) ** 0.5 * blur)
    coupled = pl.pallas_call(
        functools.partial(sinkhorn_kernel, scale),
        out_shape=jax.ShapeDtypeStruct((rows, part), jnp.float32),
        in_specs=[pl.BlockSpec(memory_space=pltpu.VMEM)] * 2,
        out_specs=pl.BlockSpec(memory_space=pltpu.VMEM),
        compiler_params=pltpu.CompilerParams(vmem_limit_bytes=16 * 2**20),
    )(cross, noise_part)
    coupled = coupled.reshape(dp_devices, row_count, part)
    coupled = lax.all_to_all(coupled, "dp", split_axis=0, concat_axis=0, tiled=True)
    target, mixed = mix(times, coupled, data, val_devices)
    moved = lax.all_to_all(mixed, val, split_axis=0, concat_axis=0, tiled=True)
    moved = moved.reshape(CH, row_count, strip)
    side = side.astype(jnp.int32).reshape(1)
    normed = embed_tokens(moved, w_patch, patch_bias, norm_gain)
    normed, w_own = lax.optimization_barrier((normed, w_own))
    w_other = lax.ppermute(w_own, "core", [(0, 1), (1, 0)])
    qkv, normed = first_half(side, normed, w_own, (256, 512, 768, 512, 256), 256)
    qkv = second_half(side, normed, w_other, qkv, (768, 768, 512, 256), 256)
    return (qkv.reshape(row_count, -1, 2 * half), target)


def solution(mesh):
    devices = mesh.devices
    fine = Mesh(devices.reshape(devices.shape[0], -1, 2), ("dp", "x", "core"))
    val = ("x", "core")
    return jax.shard_map(
        per_device,
        mesh=fine,
        in_specs=(P("dp", val), P("dp", val), P("dp"), P(), P(), P(), P("dp", None)),
        out_specs=(P("dp", val, None), P("dp", val)),
        check_vma=False,
    )
```

```python
import functools

import jax
import jax.numpy as jnp
from jax import lax
from jax.experimental import pallas as pl
from jax.experimental.pallas import tpu as pltpu
from jax.sharding import Mesh
from jax.sharding import PartitionSpec as P

CH = 16
HH = 64
WW = 64
ITERS = 4
LANES = 128


blur = 0.1


def sinkhorn_kernel(scale, cross_ref, noise_ref, coupled_ref):
    scores = cross_ref[...] * scale
    col = jnp.zeros((1, scores.shape[1]), jnp.float32)
    for step in range(ITERS):
        shifted = scores + col
        top = jnp.max(shifted, axis=1, keepdims=True)
        total = jnp.sum(jnp.exp(shifted - top), axis=1, keepdims=True)
        row = -(top + jnp.log(total))
        shifted = scores + row
        top = jnp.max(shifted, axis=0, keepdims=True)
        total = jnp.sum(jnp.exp(shifted - top), axis=0, keepdims=True)
        col = -(top + jnp.log(total))
    shifted = scores + col
    top = jnp.max(shifted, axis=1, keepdims=True)
    grown = jnp.exp(shifted - top)
    weights = (grown / jnp.sum(grown, axis=1, keepdims=True)).astype(jnp.bfloat16)
    coupled_ref[...] = jnp.dot(weights, noise_ref[...], preferred_element_type=jnp.float32)


def patch_rows(moved):
    chans, rows, wide = moved.shape
    strips = wide // LANES
    per = LANES // 4
    to = lax.broadcasted_iota(jnp.int32, (LANES, LANES), 0)
    come = lax.broadcasted_iota(jnp.int32, (LANES, LANES), 1)
    order = (come == to // (2 * per) * (2 * per) + to % per * 2 + to // per % 2).astype(jnp.bfloat16)
    flat = moved.reshape(chans * rows, wide)
    strip = []
    for p in range(strips):
        t = lax.dot_general(order, flat[:, p * LANES:(p + 1) * LANES], (((1,), (1,)), ((), ())),
                            preferred_element_type=jnp.float32).astype(jnp.bfloat16)
        strip.append(jnp.concatenate([t[f * per:(f + 1) * per] for f in range(4)], axis=1))
    strip = jnp.concatenate(strip, axis=0)
    k = strip.shape[1]
    come = lax.broadcasted_iota(jnp.int32, (k, k), 0)
    to = lax.broadcasted_iota(jnp.int32, (k, k), 1)
    f, c, r = come // (chans * rows), come // rows % chans, come % rows
    place = (to == r * (4 * chans) + c * 4 + f).astype(jnp.bfloat16)
    return jnp.dot(strip, place, preferred_element_type=jnp.float32).astype(jnp.bfloat16)

def mix_kernel(times_ref, coupled_ref, data_ref, target_ref, mixed_ref):
    count, rows, part = coupled_ref.shape
    blocks, chans, _, strip = mixed_ref.shape
    pieces = strip // part
    row = lax.broadcasted_iota(jnp.int32, (rows, part), 0)
    blend = jnp.zeros((rows, part), jnp.float32)
    for r in range(rows):
        blend = jnp.where(row == r, times_ref[r], blend)
    for k in range(count):
        chan, block, piece = k // (blocks * pieces), k // pieces % blocks, k % pieces
        coupled = coupled_ref[k]
        own = data_ref[:, k * part:(k + 1) * part].astype(jnp.float32)
        target_ref[:, k * part:(k + 1) * part] = (own - coupled).astype(jnp.bfloat16)
        mixed = (1.0 - blend) * coupled + blend * own
        mixed_ref[block, chan, :, piece * part:(piece + 1) * part] = mixed.astype(jnp.bfloat16)


def reorder(x, order):
    wide = x.shape[1] // len(order)
    return jnp.concatenate([x[:, d * wide:(d + 1) * wide] for d in order], axis=1)


def spans(widths):
    ends = [sum(widths[:t + 1]) for t in range(len(widths))]
    return [(end - width, end) for end, width in zip(ends, widths)]


def a_kernel(cols, tm, order, side_ref, moved_ref, wp_ref, bias_ref, gain_ref, w_hbm, qkv_hbm, normed,
             w_buf, out_buf, w_sem, out_sem):
    ins = [
        pltpu.make_async_copy(w_hbm.at[:, a:b], w_buf.at[:, a:b], w_sem.at[t])
        for t, (a, b) in enumerate(cols)
    ]
    for copy in ins:
        copy.start()
    chans, rows, wide = moved_ref.shape
    tok = wide // 4
    feat = 4 * chans
    w_patch = reorder(wp_ref[...].astype(jnp.float32), order).astype(jnp.bfloat16)
    bias = reorder(bias_ref[...][None, :], order)
    gain = reorder(gain_ref[...][None, :], order)
    x = patch_rows(moved_ref[...])
    for r in range(rows):
        embed = jnp.dot(x[:, r * feat:(r + 1) * feat], w_patch, preferred_element_type=jnp.float32) + bias
        center = embed - jnp.mean(embed, axis=1, keepdims=True)
        spread = jnp.mean(center * center, axis=1, keepdims=True)
        normed[r * tok:(r + 1) * tok, :] = (center * lax.rsqrt(spread + 1e-05) * gain).astype(jnp.bfloat16)
    first = side_ref[0] * w_hbm.shape[1]
    matmul(cols, tm, first, w_buf, ins, normed, out_buf, qkv_hbm, out_sem)


def matmul(cols, tm, first, w_ref, ins, normed, out_buf, qkv_hbm, out_sem):
    n_tok = normed.shape[0]
    outs = []
    for t, (a, b) in enumerate(cols):
        if ins:
            ins[t].wait()
        for m in range(0, n_tok, tm):
            out_buf[m:m + tm, a:b] = jnp.dot(
                normed[m:m + tm, :], w_ref[:, a:b], preferred_element_type=jnp.float32
            ).astype(jnp.bfloat16)
        at = pl.multiple_of(first + a, 2 * LANES)
        copy = pltpu.make_async_copy(out_buf.at[:, a:b], qkv_hbm.at[:, pl.ds(at, b - a)], out_sem.at[t])
        copy.start()
        outs.append(copy)
    for copy in outs:
        copy.wait()


def b_kernel(cols, tm, side_ref, normed, w_ref, old, qkv_hbm, out_buf, out_sem):
    first = (1 - side_ref[0]) * w_ref.shape[1]
    matmul(cols, tm, first, w_ref, None, normed, out_buf, qkv_hbm, out_sem)


def mix(times, coupled, data, blocks):
    count, rows, part = coupled.shape
    vm = pl.BlockSpec(memory_space=pltpu.VMEM)
    mixed = (blocks, CH // blocks, rows, HH // blocks * WW)
    return pl.pallas_call(
        mix_kernel,
        in_specs=[pl.BlockSpec(memory_space=pltpu.SMEM), vm, vm],
        out_specs=[vm, vm],
        out_shape=[jax.ShapeDtypeStruct(data.shape, jnp.bfloat16), jax.ShapeDtypeStruct(mixed, jnp.bfloat16)],
    )(times, coupled, data)


def first_half(side, moved, w_patch, bias, gain, w_half, order, widths, tm):
    n_tok = moved.size // w_patch.shape[0]
    hid, half = w_half.shape
    cols = spans(widths)
    vm = pl.BlockSpec(memory_space=pltpu.VMEM)
    hbm = pl.BlockSpec(memory_space=pltpu.HBM)
    return pl.pallas_call(
        functools.partial(a_kernel, cols, tm, order),
        in_specs=[pl.BlockSpec(memory_space=pltpu.SMEM), vm, vm, vm, vm, hbm],
        out_specs=[hbm, vm],
        out_shape=[
            jax.ShapeDtypeStruct((n_tok, 2 * half), jnp.bfloat16),
            jax.ShapeDtypeStruct((n_tok, hid), jnp.bfloat16),
        ],
        scratch_shapes=[
            pltpu.VMEM((hid, half), jnp.bfloat16),
            pltpu.VMEM((n_tok, half), jnp.bfloat16),
            pltpu.SemaphoreType.DMA((len(cols),)),
            pltpu.SemaphoreType.DMA((len(cols),)),
        ],
        compiler_params=pltpu.CompilerParams(vmem_limit_bytes=48 * 2**20),
        cost_estimate=pl.CostEstimate(flops=2 * n_tok * hid * half, bytes_accessed=2 * hid * half, transcendentals=0),
    )(side, moved, w_patch, bias, gain, w_half)


def second_half(side, normed, w_half, qkv, widths, tm):
    n_tok, hid = normed.shape
    half = w_half.shape[1]
    cols = spans(widths)
    vm = pl.BlockSpec(memory_space=pltpu.VMEM)
    hbm = pl.BlockSpec(memory_space=pltpu.HBM)
    return pl.pallas_call(
        functools.partial(b_kernel, cols, tm),
        in_specs=[pl.BlockSpec(memory_space=pltpu.SMEM), vm, vm, hbm],
        out_specs=hbm,
        out_shape=jax.ShapeDtypeStruct(qkv.shape, jnp.bfloat16),
        input_output_aliases={3: 0},
        scratch_shapes=[pltpu.VMEM((n_tok, half), jnp.bfloat16), pltpu.SemaphoreType.DMA((len(cols),))],
        compiler_params=pltpu.CompilerParams(vmem_limit_bytes=20 * 2**20),
        cost_estimate=pl.CostEstimate(flops=2 * n_tok * hid * half, bytes_accessed=2 * hid * half, transcendentals=0),
    )(side, normed, w_half, qkv)


def per_device(data, noise, times, w_patch, patch_bias, norm_gain, w_qkv):
    row_count, val_width = data.shape
    dp = ("y", "z")
    dp_devices = lax.axis_size(dp)
    val = ("x", "core")
    val_devices = lax.axis_size(val)
    rows = row_count * dp_devices
    part = val_width // dp_devices
    everyone = dp + val
    local_chan = CH // val_devices
    strip = HH // val_devices * WW
    pieces = strip // part
    half = w_qkv.shape[1] // 2
    side = lax.axis_index("core")
    w_own = lax.dynamic_slice_in_dim(w_qkv, side * half, half, axis=1)
    w_own = lax.all_gather(w_own, ("z", "y"), axis=0, tiled=True)
    z_size, y_size = lax.axis_size("z"), lax.axis_size("y")
    order = [y * z_size + z for z in range(z_size) for y in range(y_size)]
    pair = jnp.concatenate([data, noise], axis=0)
    pair = jnp.transpose(pair.reshape(2 * row_count, dp_devices, part), (1, 0, 2))
    pair = lax.all_to_all(pair, dp, split_axis=0, concat_axis=0, tiled=True)
    data_part = pair[:, :row_count].reshape(rows, part)
    noise_part = pair[:, row_count:].reshape(rows, part)
    cross = lax.dot_general(
        data_part, noise_part, (((1,), (1,)), ((), ())), preferred_element_type=jnp.float32
    )
    cross = cross.reshape(rows, rows // LANES, LANES)
    cross = lax.all_to_all(cross, everyone, split_axis=0, concat_axis=0, tiled=True)
    own = jnp.sum(cross, axis=0, keepdims=True)
    own = jnp.broadcast_to(own, (rows, rows // LANES, LANES))
    cross = lax.all_to_all(own, everyone, split_axis=0, concat_axis=0, tiled=True)
    cross = cross.reshape(rows, rows)
    scale = 1.0 / (float(val_width * val_devices) ** 0.5 * blur)
    coupled = pl.pallas_call(
        functools.partial(sinkhorn_kernel, scale),
        out_shape=jax.ShapeDtypeStruct((rows, part), jnp.float32),
        in_specs=[pl.BlockSpec(memory_space=pltpu.VMEM)] * 2,
        out_specs=pl.BlockSpec(memory_space=pltpu.VMEM),
        compiler_params=pltpu.CompilerParams(vmem_limit_bytes=16 * 2**20),
    )(cross, noise_part)
    coupled = coupled.reshape(dp_devices, row_count, part)
    coupled = lax.all_to_all(coupled, dp, split_axis=0, concat_axis=0, tiled=True)
    target, mixed = mix(times, coupled, data, val_devices)
    moved = lax.all_to_all(mixed, val, split_axis=0, concat_axis=0, tiled=True)
    moved = moved.reshape(CH, row_count, strip)
    side = side.astype(jnp.int32).reshape(1)
    moved, w_own = lax.optimization_barrier((moved, w_own))
    w_other = lax.ppermute(w_own, "core", [(0, 1), (1, 0)])
    qkv, normed = first_half(side, moved, w_patch, patch_bias, norm_gain, w_own, order, (256, 512, 768, 512, 256), 256)
    qkv = second_half(side, normed, w_other, qkv, (768, 768, 512, 256), 256)
    return (qkv.reshape(row_count, -1, 2 * half), target)


def solution(mesh):
    dp, val = ("y", "z"), ("x", "core")
    fine = Mesh(mesh.devices.reshape(4, 8, -1, 2), dp + val)
    return jax.shard_map(
        per_device,
        mesh=fine,
        in_specs=(P(dp, val), P(dp, val), P(dp), P(), P(), P(), P(dp, None)),
        out_specs=(P(dp, val, None), P(dp, val)),
        check_vma=False,
    )
```

```python
import functools

import jax
import jax.numpy as jnp
from jax import lax
from jax.experimental import pallas as pl
from jax.experimental.pallas import tpu as pltpu
from jax.sharding import Mesh
from jax.sharding import PartitionSpec as P

CH = 16
HH = 64
WW = 64
ITERS = 4
LANES = 128


blur = 0.1


def sinkhorn_kernel(scale, cross_ref, noise_ref, coupled_ref):
    scores = cross_ref[...] * scale
    col = jnp.zeros((1, scores.shape[1]), jnp.float32)
    for step in range(ITERS):
        shifted = scores + col
        top = jnp.max(shifted, axis=1, keepdims=True)
        total = jnp.sum(jnp.exp(shifted - top), axis=1, keepdims=True)
        row = -(top + jnp.log(total))
        shifted = scores + row
        top = jnp.max(shifted, axis=0, keepdims=True)
        total = jnp.sum(jnp.exp(shifted - top), axis=0, keepdims=True)
        col = -(top + jnp.log(total))
    shifted = scores + col
    top = jnp.max(shifted, axis=1, keepdims=True)
    grown = jnp.exp(shifted - top)
    weights = (grown / jnp.sum(grown, axis=1, keepdims=True)).astype(jnp.bfloat16)
    coupled_ref[...] = jnp.dot(weights, noise_ref[...], preferred_element_type=jnp.float32)


def patch_rows(moved):
    chans, rows, wide = moved.shape
    strips = wide // LANES
    per = LANES // 4
    to = lax.broadcasted_iota(jnp.int32, (LANES, LANES), 0)
    come = lax.broadcasted_iota(jnp.int32, (LANES, LANES), 1)
    order = (come == to // (2 * per) * (2 * per) + to % per * 2 + to // per % 2).astype(jnp.bfloat16)
    flat = moved.reshape(chans * rows, wide)
    strip = []
    for p in range(strips):
        t = lax.dot_general(order, flat[:, p * LANES:(p + 1) * LANES], (((1,), (1,)), ((), ())),
                            preferred_element_type=jnp.float32).astype(jnp.bfloat16)
        strip.append(jnp.concatenate([t[f * per:(f + 1) * per] for f in range(4)], axis=1))
    strip = jnp.concatenate(strip, axis=0)
    k = strip.shape[1]
    come = lax.broadcasted_iota(jnp.int32, (k, k), 0)
    to = lax.broadcasted_iota(jnp.int32, (k, k), 1)
    f, c, r = come // (chans * rows), come // rows % chans, come % rows
    place = (to == r * (4 * chans) + c * 4 + f).astype(jnp.bfloat16)
    return jnp.dot(strip, place, preferred_element_type=jnp.float32).astype(jnp.bfloat16)

def mix_kernel(times_ref, coupled_ref, data_ref, target_ref, mixed_ref):
    count, rows, part = coupled_ref.shape
    blocks, chans, _, strip = mixed_ref.shape
    pieces = strip // part
    row = lax.broadcasted_iota(jnp.int32, (rows, part), 0)
    blend = jnp.zeros((rows, part), jnp.float32)
    for r in range(rows):
        blend = jnp.where(row == r, times_ref[r], blend)
    for k in range(count):
        chan, block, piece = k // (blocks * pieces), k // pieces % blocks, k % pieces
        coupled = coupled_ref[k]
        own = data_ref[:, k * part:(k + 1) * part].astype(jnp.float32)
        target_ref[:, k * part:(k + 1) * part] = (own - coupled).astype(jnp.bfloat16)
        mixed = (1.0 - blend) * coupled + blend * own
        mixed_ref[block, chan, :, piece * part:(piece + 1) * part] = mixed.astype(jnp.bfloat16)


def spans(widths):
    ends = [sum(widths[:t + 1]) for t in range(len(widths))]
    return [(end - width, end) for end, width in zip(ends, widths)]


def project_kernel(cols, tm, moved_ref, wp_ref, bias_ref, gain_ref, w_hbm, qkv_hbm, normed, w_buf, out_buf, w_sem, out_sem):
    ins = [
        pltpu.make_async_copy(w_hbm.at[:, c, :, a:b], w_buf.at[c, :, :, a:b], w_sem.at[t])
        for t, (c, a, b) in enumerate(cols)
    ]
    for copy in ins:
        copy.start()
    chans, rows, wide = moved_ref.shape
    tok = wide // 4
    feat = 4 * chans
    x = patch_rows(moved_ref[...])
    for r in range(rows):
        embed = jnp.dot(x[:, r * feat:(r + 1) * feat], wp_ref[...], preferred_element_type=jnp.float32) + bias_ref[...][None, :]
        center = embed - jnp.mean(embed, axis=1, keepdims=True)
        spread = jnp.mean(center * center, axis=1, keepdims=True)
        normed[r * tok:(r + 1) * tok, :] = (center * lax.rsqrt(spread + 1e-05) * gain_ref[...][None, :]).astype(jnp.bfloat16)
    n_tok, hid = normed.shape
    half = w_hbm.shape[3]
    outs = []
    for t, (c, a, b) in enumerate(cols):
        ins[t].wait()
        for m in range(0, n_tok, tm):
            w = w_buf[c, :, :, a:b].reshape(hid, b - a)
            out_buf[m:m + tm, c * half + a:c * half + b] = jnp.dot(
                normed[m:m + tm, :], w, preferred_element_type=jnp.float32
            ).astype(jnp.bfloat16)
        at = slice(c * half + a, c * half + b)
        copy = pltpu.make_async_copy(out_buf.at[:, at], qkv_hbm.at[:, at], out_sem.at[t])
        copy.start()
        outs.append(copy)
    for copy in outs:
        copy.wait()


def mix(times, coupled, data, blocks):
    count, rows, part = coupled.shape
    vm = pl.BlockSpec(memory_space=pltpu.VMEM)
    mixed = (blocks, CH // blocks, rows, HH // blocks * WW)
    return pl.pallas_call(
        mix_kernel,
        in_specs=[pl.BlockSpec(memory_space=pltpu.SMEM), vm, vm],
        out_specs=[vm, vm],
        out_shape=[jax.ShapeDtypeStruct(data.shape, jnp.bfloat16), jax.ShapeDtypeStruct(mixed, jnp.bfloat16)],
    )(times, coupled, data)


def project(moved, w_patch, bias, gain, w, first_widths, last_widths, tm):
    n_tok = moved.size // w_patch.shape[0]
    blocks, halves, depth, half = w.shape
    hid = blocks * depth
    cols = [(0, a, b) for a, b in spans(first_widths)] + [(1, a, b) for a, b in spans(last_widths)]
    vm = pl.BlockSpec(memory_space=pltpu.VMEM)
    hbm = pl.BlockSpec(memory_space=pltpu.HBM)
    return pl.pallas_call(
        functools.partial(project_kernel, cols, tm),
        in_specs=[vm, vm, vm, vm, hbm],
        out_specs=hbm,
        out_shape=jax.ShapeDtypeStruct((n_tok, halves * half), jnp.bfloat16),
        scratch_shapes=[
            pltpu.VMEM((n_tok, hid), jnp.bfloat16),
            pltpu.VMEM((halves, blocks, depth, half), jnp.bfloat16),
            pltpu.VMEM((n_tok, halves * half), jnp.bfloat16),
            pltpu.SemaphoreType.DMA((len(cols),)),
            pltpu.SemaphoreType.DMA((len(cols),)),
        ],
        compiler_params=pltpu.CompilerParams(vmem_limit_bytes=50 * 2**20),
        cost_estimate=pl.CostEstimate(flops=4 * n_tok * hid * half, bytes_accessed=4 * hid * half, transcendentals=0),
    )(moved, w_patch, bias, gain, w)


def per_device(data, noise, times, w_patch, patch_bias, norm_gain, w_qkv):
    row_count, val_width = data.shape
    dp = ("y", "z")
    dp_devices = lax.axis_size(dp)
    val = ("x", "core")
    val_devices = lax.axis_size(val)
    rows = row_count * dp_devices
    part = val_width // dp_devices
    everyone = dp + val
    local_chan = CH // val_devices
    strip = HH // val_devices * WW
    pieces = strip // part
    half = w_qkv.shape[1] // 2
    side = lax.axis_index("core")
    w_own = lax.dynamic_slice_in_dim(w_qkv, side * half, half, axis=1)
    w = lax.all_gather(w_own, dp + ("core",), axis=0, tiled=False)
    w = w.reshape(dp_devices, 2, w_qkv.shape[0], half)
    pair = jnp.concatenate([data, noise], axis=0)
    pair = jnp.transpose(pair.reshape(2 * row_count, dp_devices, part), (1, 0, 2))
    pair = lax.all_to_all(pair, dp, split_axis=0, concat_axis=0, tiled=True)
    data_part = pair[:, :row_count].reshape(rows, part)
    noise_part = pair[:, row_count:].reshape(rows, part)
    cross = lax.dot_general(
        data_part, noise_part, (((1,), (1,)), ((), ())), preferred_element_type=jnp.float32
    )
    cross = cross.reshape(rows, rows // LANES, LANES)
    cross = lax.all_to_all(cross, everyone, split_axis=0, concat_axis=0, tiled=True)
    own = jnp.sum(cross, axis=0, keepdims=True)
    own = jnp.broadcast_to(own, (rows, rows // LANES, LANES))
    cross = lax.all_to_all(own, everyone, split_axis=0, concat_axis=0, tiled=True)
    cross = cross.reshape(rows, rows)
    scale = 1.0 / (float(val_width * val_devices) ** 0.5 * blur)
    coupled = pl.pallas_call(
        functools.partial(sinkhorn_kernel, scale),
        out_shape=jax.ShapeDtypeStruct((rows, part), jnp.float32),
        in_specs=[pl.BlockSpec(memory_space=pltpu.VMEM)] * 2,
        out_specs=pl.BlockSpec(memory_space=pltpu.VMEM),
        compiler_params=pltpu.CompilerParams(vmem_limit_bytes=16 * 2**20),
    )(cross, noise_part)
    coupled = coupled.reshape(dp_devices, row_count, part)
    coupled = lax.all_to_all(coupled, dp, split_axis=0, concat_axis=0, tiled=True)
    target, mixed = mix(times, coupled, data, val_devices)
    moved = lax.all_to_all(mixed, val, split_axis=0, concat_axis=0, tiled=True)
    moved = moved.reshape(CH, row_count, strip)
    qkv = project(moved, w_patch, patch_bias, norm_gain, w, (256, 512, 768, 768), (768, 768, 512, 256), 256)
    return (qkv.reshape(row_count, -1, 2 * half), target)


def solution(mesh):
    dp, val = ("y", "z"), ("x", "core")
    fine = Mesh(mesh.devices.reshape(4, 8, -1, 2), dp + val)
    return jax.shard_map(
        per_device,
        mesh=fine,
        in_specs=(P(dp, val), P(dp, val), P(dp), P(), P(), P(), P(dp, None)),
        out_specs=(P(dp, val, None), P(dp, val)),
        check_vma=False,
    )
```

```python
import functools

import jax
import jax.numpy as jnp
from jax import lax
from jax.experimental import pallas as pl
from jax.experimental.pallas import tpu as pltpu
from jax.sharding import Mesh
from jax.sharding import PartitionSpec as P

CH = 16
HH = 64
WW = 64
ITERS = 4
LANES = 128


blur = 0.1


def sinkhorn_kernel(scale, cross_ref, noise_ref, coupled_ref):
    scores = cross_ref[...] * scale
    col = jnp.zeros((1, scores.shape[1]), jnp.float32)
    for step in range(ITERS):
        shifted = scores + col
        top = jnp.max(shifted, axis=1, keepdims=True)
        total = jnp.sum(jnp.exp(shifted - top), axis=1, keepdims=True)
        row = -(top + jnp.log(total))
        shifted = scores + row
        top = jnp.max(shifted, axis=0, keepdims=True)
        total = jnp.sum(jnp.exp(shifted - top), axis=0, keepdims=True)
        col = -(top + jnp.log(total))
    shifted = scores + col
    top = jnp.max(shifted, axis=1, keepdims=True)
    grown = jnp.exp(shifted - top)
    weights = (grown / jnp.sum(grown, axis=1, keepdims=True)).astype(jnp.bfloat16)
    coupled_ref[...] = jnp.dot(weights, noise_ref[...], preferred_element_type=jnp.float32)


def patch_rows(moved):
    chans, rows, wide = moved.shape
    strips = wide // LANES
    per = LANES // 4
    to = lax.broadcasted_iota(jnp.int32, (LANES, LANES), 0)
    come = lax.broadcasted_iota(jnp.int32, (LANES, LANES), 1)
    order = (come == to // (2 * per) * (2 * per) + to % per * 2 + to // per % 2).astype(jnp.bfloat16)
    flat = moved.reshape(chans * rows, wide)
    strip = []
    for p in range(strips):
        t = lax.dot_general(order, flat[:, p * LANES:(p + 1) * LANES], (((1,), (1,)), ((), ())),
                            preferred_element_type=jnp.float32).astype(jnp.bfloat16)
        strip.append(jnp.concatenate([t[f * per:(f + 1) * per] for f in range(4)], axis=1))
    strip = jnp.concatenate(strip, axis=0)
    k = strip.shape[1]
    come = lax.broadcasted_iota(jnp.int32, (k, k), 0)
    to = lax.broadcasted_iota(jnp.int32, (k, k), 1)
    f, c, r = come // (chans * rows), come // rows % chans, come % rows
    place = (to == r * (4 * chans) + c * 4 + f).astype(jnp.bfloat16)
    return jnp.dot(strip, place, preferred_element_type=jnp.float32).astype(jnp.bfloat16)

def mix_kernel(times_ref, coupled_ref, data_ref, target_ref, mixed_ref):
    count, rows, part = coupled_ref.shape
    blocks, chans, _, strip = mixed_ref.shape
    pieces = strip // part
    row = lax.broadcasted_iota(jnp.int32, (rows, part), 0)
    blend = jnp.zeros((rows, part), jnp.float32)
    for r in range(rows):
        blend = jnp.where(row == r, times_ref[r], blend)
    for k in range(count):
        chan, block, piece = k // (blocks * pieces), k // pieces % blocks, k % pieces
        coupled = coupled_ref[k]
        own = data_ref[:, k * part:(k + 1) * part].astype(jnp.float32)
        target_ref[:, k * part:(k + 1) * part] = (own - coupled).astype(jnp.bfloat16)
        mixed = (1.0 - blend) * coupled + blend * own
        mixed_ref[block, chan, :, piece * part:(piece + 1) * part] = mixed.astype(jnp.bfloat16)


def reorder(x, order):
    wide = x.shape[1] // len(order)
    return jnp.concatenate([x[:, d * wide:(d + 1) * wide] for d in order], axis=1)


def spans(widths):
    ends = [sum(widths[:t + 1]) for t in range(len(widths))]
    return [(end - width, end) for end, width in zip(ends, widths)]


def a_kernel(cols, tm, order, side_ref, moved_ref, wp_ref, bias_ref, gain_ref, w_hbm, qkv_hbm, normed,
             w_buf, out_buf, w_sem, out_sem):
    ins = [
        pltpu.make_async_copy(w_hbm.at[:, a:b], w_buf.at[:, a:b], w_sem.at[t])
        for t, (a, b) in enumerate(cols)
    ]
    for copy in ins:
        copy.start()
    chans, rows, wide = moved_ref.shape
    tok = wide // 4
    feat = 4 * chans
    w_patch = reorder(wp_ref[...].astype(jnp.float32), order).astype(jnp.bfloat16)
    bias = reorder(bias_ref[...][None, :], order)
    gain = reorder(gain_ref[...][None, :], order)
    x = patch_rows(moved_ref[...])
    for r in range(rows):
        embed = jnp.dot(x[:, r * feat:(r + 1) * feat], w_patch, preferred_element_type=jnp.float32) + bias
        center = embed - jnp.mean(embed, axis=1, keepdims=True)
        spread = jnp.mean(center * center, axis=1, keepdims=True)
        normed[r * tok:(r + 1) * tok, :] = (center * lax.rsqrt(spread + 1e-05) * gain).astype(jnp.bfloat16)
    first = side_ref[0] * w_hbm.shape[1]
    matmul(cols, tm, first, w_buf, ins, normed, out_buf, qkv_hbm, out_sem)


def matmul(cols, tm, first, w_ref, ins, normed, out_buf, qkv_hbm, out_sem):
    n_tok = normed.shape[0]
    outs = []
    for t, (a, b) in enumerate(cols):
        if ins:
            ins[t].wait()
        for m in range(0, n_tok, tm):
            out_buf[m:m + tm, a:b] = jnp.dot(
                normed[m:m + tm, :], w_ref[:, a:b], preferred_element_type=jnp.float32
            ).astype(jnp.bfloat16)
        at = pl.multiple_of(first + a, 2 * LANES)
        copy = pltpu.make_async_copy(out_buf.at[:, a:b], qkv_hbm.at[:, pl.ds(at, b - a)], out_sem.at[t])
        copy.start()
        outs.append(copy)
    for copy in outs:
        copy.wait()


def b_kernel(cols, tm, side_ref, normed, w_ref, old, qkv_hbm, out_buf, out_sem):
    first = (1 - side_ref[0]) * w_ref.shape[1]
    matmul(cols, tm, first, w_ref, None, normed, out_buf, qkv_hbm, out_sem)


def mix(times, coupled, data, blocks):
    count, rows, part = coupled.shape
    vm = pl.BlockSpec(memory_space=pltpu.VMEM)
    mixed = (blocks, CH // blocks, rows, HH // blocks * WW)
    return pl.pallas_call(
        mix_kernel,
        in_specs=[pl.BlockSpec(memory_space=pltpu.SMEM), vm, vm],
        out_specs=[vm, vm],
        out_shape=[jax.ShapeDtypeStruct(data.shape, jnp.bfloat16), jax.ShapeDtypeStruct(mixed, jnp.bfloat16)],
    )(times, coupled, data)


def first_half(side, moved, w_patch, bias, gain, w_half, order, widths, tm):
    n_tok = moved.size // w_patch.shape[0]
    hid, half = w_half.shape
    cols = spans(widths)
    vm = pl.BlockSpec(memory_space=pltpu.VMEM)
    hbm = pl.BlockSpec(memory_space=pltpu.HBM)
    return pl.pallas_call(
        functools.partial(a_kernel, cols, tm, order),
        in_specs=[pl.BlockSpec(memory_space=pltpu.SMEM), vm, vm, vm, vm, hbm],
        out_specs=[hbm, vm],
        out_shape=[
            jax.ShapeDtypeStruct((n_tok, 2 * half), jnp.bfloat16),
            jax.ShapeDtypeStruct((n_tok, hid), jnp.bfloat16),
        ],
        scratch_shapes=[
            pltpu.VMEM((hid, half), jnp.bfloat16),
            pltpu.VMEM((n_tok, half), jnp.bfloat16),
            pltpu.SemaphoreType.DMA((len(cols),)),
            pltpu.SemaphoreType.DMA((len(cols),)),
        ],
        compiler_params=pltpu.CompilerParams(vmem_limit_bytes=48 * 2**20),
        cost_estimate=pl.CostEstimate(flops=2 * n_tok * hid * half, bytes_accessed=2 * hid * half, transcendentals=0),
    )(side, moved, w_patch, bias, gain, w_half)


def second_half(side, normed, w_half, qkv, widths, tm):
    n_tok, hid = normed.shape
    half = w_half.shape[1]
    cols = spans(widths)
    vm = pl.BlockSpec(memory_space=pltpu.VMEM)
    hbm = pl.BlockSpec(memory_space=pltpu.HBM)
    return pl.pallas_call(
        functools.partial(b_kernel, cols, tm),
        in_specs=[pl.BlockSpec(memory_space=pltpu.SMEM), vm, vm, hbm],
        out_specs=hbm,
        out_shape=jax.ShapeDtypeStruct(qkv.shape, jnp.bfloat16),
        input_output_aliases={3: 0},
        scratch_shapes=[pltpu.VMEM((n_tok, half), jnp.bfloat16), pltpu.SemaphoreType.DMA((len(cols),))],
        compiler_params=pltpu.CompilerParams(vmem_limit_bytes=20 * 2**20),
        cost_estimate=pl.CostEstimate(flops=2 * n_tok * hid * half, bytes_accessed=2 * hid * half, transcendentals=0),
    )(side, normed, w_half, qkv)


def per_device(data, noise, times, w_patch, patch_bias, norm_gain, w_qkv):
    row_count, val_width = data.shape
    dp = ("y", "z")
    dp_devices = lax.axis_size(dp)
    val = ("x", "core")
    val_devices = lax.axis_size(val)
    rows = row_count * dp_devices
    part = val_width // dp_devices
    everyone = dp + val
    local_chan = CH // val_devices
    strip = HH // val_devices * WW
    pieces = strip // part
    half = w_qkv.shape[1] // 2
    side = lax.axis_index("core")
    w_own = lax.dynamic_slice_in_dim(w_qkv, side * half, half, axis=1)
    w_own = lax.all_gather(w_own, ("z", "y"), axis=0, tiled=True)
    z_size, y_size = lax.axis_size("z"), lax.axis_size("y")
    order = [y * z_size + z for z in range(z_size) for y in range(y_size)]
    pair = jnp.concatenate([data, noise], axis=0)
    pair = jnp.transpose(pair.reshape(2 * row_count, dp_devices, part), (1, 0, 2))
    pair = lax.all_to_all(pair, dp, split_axis=0, concat_axis=0, tiled=True)
    data_part = pair[:, :row_count].reshape(rows, part)
    noise_part = pair[:, row_count:].reshape(rows, part)
    cross = lax.dot_general(
        data_part, noise_part, (((1,), (1,)), ((), ())), preferred_element_type=jnp.float32
    )
    chips = dp + ("x",)
    swap = [(0, 1), (1, 0)]
    group = rows // 2
    away = lax.dynamic_slice_in_dim(cross, (1 - side) * group, group, axis=0)
    kept = lax.dynamic_slice_in_dim(cross, side * group, group, axis=0)
    cross = kept + lax.ppermute(away, "core", swap)
    cross = cross.reshape(group, rows // LANES, LANES)
    cross = lax.all_to_all(cross, chips, split_axis=0, concat_axis=0, tiled=True)
    own = jnp.sum(cross, axis=0, keepdims=True)
    own = jnp.broadcast_to(own, (group, rows // LANES, LANES))
    cross = lax.all_to_all(own, chips, split_axis=0, concat_axis=0, tiled=True)
    cross = cross.reshape(group, rows)
    other = lax.ppermute(cross, "core", swap)
    upper = jnp.where(side == 0, cross, other)
    lower = jnp.where(side == 0, other, cross)
    cross = jnp.concatenate([upper, lower], axis=0)
    scale = 1.0 / (float(val_width * val_devices) ** 0.5 * blur)
    coupled = pl.pallas_call(
        functools.partial(sinkhorn_kernel, scale),
        out_shape=jax.ShapeDtypeStruct((rows, part), jnp.float32),
        in_specs=[pl.BlockSpec(memory_space=pltpu.VMEM)] * 2,
        out_specs=pl.BlockSpec(memory_space=pltpu.VMEM),
        compiler_params=pltpu.CompilerParams(vmem_limit_bytes=16 * 2**20),
    )(cross, noise_part)
    coupled = coupled.reshape(dp_devices, row_count, part)
    coupled = lax.all_to_all(coupled, dp, split_axis=0, concat_axis=0, tiled=True)
    target, mixed = mix(times, coupled, data, val_devices)
    moved = lax.all_to_all(mixed, val, split_axis=0, concat_axis=0, tiled=True)
    moved = moved.reshape(CH, row_count, strip)
    side = side.astype(jnp.int32).reshape(1)
    moved, w_own = lax.optimization_barrier((moved, w_own))
    w_other = lax.ppermute(w_own, "core", [(0, 1), (1, 0)])
    qkv, normed = first_half(side, moved, w_patch, patch_bias, norm_gain, w_own, order, (256, 512, 768, 512, 256), 256)
    qkv = second_half(side, normed, w_other, qkv, (768, 768, 512, 256), 256)
    return (qkv.reshape(row_count, -1, 2 * half), target)


def solution(mesh):
    dp, val = ("y", "z"), ("x", "core")
    fine = Mesh(mesh.devices.reshape(4, 8, -1, 2), dp + val)
    return jax.shard_map(
        per_device,
        mesh=fine,
        in_specs=(P(dp, val), P(dp, val), P(dp), P(), P(), P(), P(dp, None)),
        out_specs=(P(dp, val, None), P(dp, val)),
        check_vma=False,
    )
```

```python
import functools

import jax
import jax.numpy as jnp
from jax import lax
from jax.experimental import pallas as pl
from jax.experimental.pallas import tpu as pltpu
from jax.sharding import Mesh
from jax.sharding import PartitionSpec as P

CH = 16
HH = 64
WW = 64
ITERS = 4
LANES = 128


blur = 0.1


def sinkhorn_kernel(scale, cross_ref, noise_ref, coupled_ref):
    scores = cross_ref[...] * scale
    col = jnp.zeros((1, scores.shape[1]), jnp.float32)
    for step in range(ITERS):
        shifted = scores + col
        top = jnp.max(shifted, axis=1, keepdims=True)
        total = jnp.sum(jnp.exp(shifted - top), axis=1, keepdims=True)
        row = -(top + jnp.log(total))
        shifted = scores + row
        top = jnp.max(shifted, axis=0, keepdims=True)
        total = jnp.sum(jnp.exp(shifted - top), axis=0, keepdims=True)
        col = -(top + jnp.log(total))
    shifted = scores + col
    top = jnp.max(shifted, axis=1, keepdims=True)
    grown = jnp.exp(shifted - top)
    weights = (grown / jnp.sum(grown, axis=1, keepdims=True)).astype(jnp.bfloat16)
    coupled_ref[...] = jnp.dot(weights, noise_ref[...], preferred_element_type=jnp.float32)


def patch_rows(moved):
    chans, rows, wide = moved.shape
    strips = wide // LANES
    per = LANES // 4
    to = lax.broadcasted_iota(jnp.int32, (LANES, LANES), 0)
    come = lax.broadcasted_iota(jnp.int32, (LANES, LANES), 1)
    order = (come == to // (2 * per) * (2 * per) + to % per * 2 + to // per % 2).astype(jnp.bfloat16)
    flat = moved.reshape(chans * rows, wide)
    strip = []
    for p in range(strips):
        t = lax.dot_general(order, flat[:, p * LANES:(p + 1) * LANES], (((1,), (1,)), ((), ())),
                            preferred_element_type=jnp.float32).astype(jnp.bfloat16)
        strip.append(jnp.concatenate([t[f * per:(f + 1) * per] for f in range(4)], axis=1))
    strip = jnp.concatenate(strip, axis=0)
    k = strip.shape[1]
    come = lax.broadcasted_iota(jnp.int32, (k, k), 0)
    to = lax.broadcasted_iota(jnp.int32, (k, k), 1)
    f, c, r = come // (chans * rows), come // rows % chans, come % rows
    place = (to == r * (4 * chans) + c * 4 + f).astype(jnp.bfloat16)
    return jnp.dot(strip, place, preferred_element_type=jnp.float32).astype(jnp.bfloat16)

def mix_kernel(times_ref, coupled_ref, data_ref, target_ref, mixed_ref):
    count, rows, part = coupled_ref.shape
    blocks, chans, _, strip = mixed_ref.shape
    pieces = strip // part
    row = lax.broadcasted_iota(jnp.int32, (rows, part), 0)
    blend = jnp.zeros((rows, part), jnp.float32)
    for r in range(rows):
        blend = jnp.where(row == r, times_ref[r], blend)
    for k in range(count):
        chan, block, piece = k // (blocks * pieces), k // pieces % blocks, k % pieces
        coupled = coupled_ref[k]
        own = data_ref[:, k * part:(k + 1) * part].astype(jnp.float32)
        target_ref[:, k * part:(k + 1) * part] = (own - coupled).astype(jnp.bfloat16)
        mixed = (1.0 - blend) * coupled + blend * own
        mixed_ref[block, chan, :, piece * part:(piece + 1) * part] = mixed.astype(jnp.bfloat16)


def reorder(x, order):
    wide = x.shape[1] // len(order)
    return jnp.concatenate([x[:, d * wide:(d + 1) * wide] for d in order], axis=1)


def spans(widths):
    ends = [sum(widths[:t + 1]) for t in range(len(widths))]
    return [(end - width, end) for end, width in zip(ends, widths)]


def stats_kernel(order, moved_ref, wp_ref, bias_ref, gain_ref, x_ref, stats_ref, w_ref, scale_ref):
    chans, rows, wide = moved_ref.shape
    tok = wide // 4
    feat = 4 * chans
    w_patch = reorder(wp_ref[...].astype(jnp.float32), order).astype(jnp.bfloat16)
    bias = reorder(bias_ref[...][None, :], order)
    gain = reorder(gain_ref[...][None, :], order)
    w_ref[...] = w_patch
    scale_ref[0:1, :] = bias
    scale_ref[1:2, :] = gain
    x = patch_rows(moved_ref[...])
    x_ref[...] = x
    for r in range(rows):
        embed = jnp.dot(x[:, r * feat:(r + 1) * feat], w_patch, preferred_element_type=jnp.float32) + bias
        mean = jnp.mean(embed, axis=1, keepdims=True)
        center = embed - mean
        spread = jnp.mean(center * center, axis=1, keepdims=True)
        stats_ref[r * tok:(r + 1) * tok, 0:1] = mean
        stats_ref[r * tok:(r + 1) * tok, 1:2] = lax.rsqrt(spread + 1e-05)


def a_kernel(cols, tm, side_ref, x_ref, stats_ref, wp_ref, scale_ref, w_hbm, qkv_hbm, normed,
             w_buf, out_buf, w_sem, out_sem):
    ins = [
        pltpu.make_async_copy(w_hbm.at[:, a:b], w_buf.at[:, a:b], w_sem.at[t])
        for t, (a, b) in enumerate(cols)
    ]
    for copy in ins:
        copy.start()
    tok = x_ref.shape[0]
    feat = wp_ref.shape[0]
    bias, gain = scale_ref[0:1, :], scale_ref[1:2, :]
    for r in range(normed.shape[0] // tok):
        embed = jnp.dot(x_ref[:, r * feat:(r + 1) * feat], wp_ref[...], preferred_element_type=jnp.float32) + bias
        at = slice(r * tok, (r + 1) * tok)
        normed[at, :] = ((embed - stats_ref[at, 0:1]) * stats_ref[at, 1:2] * gain).astype(jnp.bfloat16)
    first = side_ref[0] * w_hbm.shape[1]
    matmul(cols, tm, first, w_buf, ins, normed, out_buf, qkv_hbm, out_sem)


def matmul(cols, tm, first, w_ref, ins, normed, out_buf, qkv_hbm, out_sem):
    n_tok = normed.shape[0]
    outs = []
    for t, (a, b) in enumerate(cols):
        if ins:
            ins[t].wait()
        for m in range(0, n_tok, tm):
            out_buf[m:m + tm, a:b] = jnp.dot(
                normed[m:m + tm, :], w_ref[:, a:b], preferred_element_type=jnp.float32
            ).astype(jnp.bfloat16)
        at = pl.multiple_of(first + a, 2 * LANES)
        copy = pltpu.make_async_copy(out_buf.at[:, a:b], qkv_hbm.at[:, pl.ds(at, b - a)], out_sem.at[t])
        copy.start()
        outs.append(copy)
    for copy in outs:
        copy.wait()


def b_kernel(cols, tm, side_ref, normed, w_ref, old, qkv_hbm, out_buf, out_sem):
    first = (1 - side_ref[0]) * w_ref.shape[1]
    matmul(cols, tm, first, w_ref, None, normed, out_buf, qkv_hbm, out_sem)


def mix(times, coupled, data, blocks):
    count, rows, part = coupled.shape
    vm = pl.BlockSpec(memory_space=pltpu.VMEM)
    mixed = (blocks, CH // blocks, rows, HH // blocks * WW)
    return pl.pallas_call(
        mix_kernel,
        in_specs=[pl.BlockSpec(memory_space=pltpu.SMEM), vm, vm],
        out_specs=[vm, vm],
        out_shape=[jax.ShapeDtypeStruct(data.shape, jnp.bfloat16), jax.ShapeDtypeStruct(mixed, jnp.bfloat16)],
    )(times, coupled, data)


def token_stats(moved, w_patch, bias, gain, order):
    feat, hid = w_patch.shape
    chans, rows, wide = moved.shape
    tok = wide // 4
    vm = pl.BlockSpec(memory_space=pltpu.VMEM)
    return pl.pallas_call(
        functools.partial(stats_kernel, order),
        in_specs=[vm] * 4,
        out_specs=[vm] * 4,
        out_shape=[
            jax.ShapeDtypeStruct((tok, rows * feat), jnp.bfloat16),
            jax.ShapeDtypeStruct((rows * tok, 2), jnp.float32),
            jax.ShapeDtypeStruct((feat, hid), jnp.bfloat16),
            jax.ShapeDtypeStruct((2, hid), jnp.float32),
        ],
        compiler_params=pltpu.CompilerParams(vmem_limit_bytes=48 * 2**20),
    )(moved, w_patch, bias, gain)


def first_half(side, x, stats, w_patch, scales, w_half, widths, tm):
    n_tok = stats.shape[0]
    hid, half = w_half.shape
    cols = spans(widths)
    vm = pl.BlockSpec(memory_space=pltpu.VMEM)
    hbm = pl.BlockSpec(memory_space=pltpu.HBM)
    return pl.pallas_call(
        functools.partial(a_kernel, cols, tm),
        in_specs=[pl.BlockSpec(memory_space=pltpu.SMEM), vm, vm, vm, vm, hbm],
        out_specs=[hbm, vm],
        out_shape=[
            jax.ShapeDtypeStruct((n_tok, 2 * half), jnp.bfloat16),
            jax.ShapeDtypeStruct((n_tok, hid), jnp.bfloat16),
        ],
        scratch_shapes=[
            pltpu.VMEM((hid, half), jnp.bfloat16),
            pltpu.VMEM((n_tok, half), jnp.bfloat16),
            pltpu.SemaphoreType.DMA((len(cols),)),
            pltpu.SemaphoreType.DMA((len(cols),)),
        ],
        compiler_params=pltpu.CompilerParams(vmem_limit_bytes=48 * 2**20),
        cost_estimate=pl.CostEstimate(flops=2 * n_tok * hid * half, bytes_accessed=2 * hid * half, transcendentals=0),
    )(side, x, stats, w_patch, scales, w_half)


def second_half(side, normed, w_half, qkv, widths, tm):
    n_tok, hid = normed.shape
    half = w_half.shape[1]
    cols = spans(widths)
    vm = pl.BlockSpec(memory_space=pltpu.VMEM)
    hbm = pl.BlockSpec(memory_space=pltpu.HBM)
    return pl.pallas_call(
        functools.partial(b_kernel, cols, tm),
        in_specs=[pl.BlockSpec(memory_space=pltpu.SMEM), vm, vm, hbm],
        out_specs=hbm,
        out_shape=jax.ShapeDtypeStruct(qkv.shape, jnp.bfloat16),
        input_output_aliases={3: 0},
        scratch_shapes=[pltpu.VMEM((n_tok, half), jnp.bfloat16), pltpu.SemaphoreType.DMA((len(cols),))],
        compiler_params=pltpu.CompilerParams(vmem_limit_bytes=20 * 2**20),
        cost_estimate=pl.CostEstimate(flops=2 * n_tok * hid * half, bytes_accessed=2 * hid * half, transcendentals=0),
    )(side, normed, w_half, qkv)


def per_device(data, noise, times, w_patch, patch_bias, norm_gain, w_qkv):
    row_count, val_width = data.shape
    dp = ("y", "z")
    dp_devices = lax.axis_size(dp)
    val = ("x", "core")
    val_devices = lax.axis_size(val)
    rows = row_count * dp_devices
    part = val_width // dp_devices
    everyone = dp + val
    local_chan = CH // val_devices
    strip = HH // val_devices * WW
    pieces = strip // part
    half = w_qkv.shape[1] // 2
    side = lax.axis_index("core")
    w_own = lax.dynamic_slice_in_dim(w_qkv, side * half, half, axis=1)
    w_own = lax.all_gather(w_own, ("z", "y"), axis=0, tiled=True)
    z_size, y_size = lax.axis_size("z"), lax.axis_size("y")
    order = [y * z_size + z for z in range(z_size) for y in range(y_size)]
    pair = jnp.concatenate([data, noise], axis=0)
    pair = jnp.transpose(pair.reshape(2 * row_count, dp_devices, part), (1, 0, 2))
    pair = lax.all_to_all(pair, dp, split_axis=0, concat_axis=0, tiled=True)
    data_part = pair[:, :row_count].reshape(rows, part)
    noise_part = pair[:, row_count:].reshape(rows, part)
    cross = lax.dot_general(
        data_part, noise_part, (((1,), (1,)), ((), ())), preferred_element_type=jnp.float32
    )
    chips = dp + ("x",)
    swap = [(0, 1), (1, 0)]
    group = rows // 2
    away = lax.dynamic_slice_in_dim(cross, (1 - side) * group, group, axis=0)
    kept = lax.dynamic_slice_in_dim(cross, side * group, group, axis=0)
    cross = kept + lax.ppermute(away, "core", swap)
    cross = cross.reshape(group, rows // LANES, LANES)
    cross = lax.all_to_all(cross, chips, split_axis=0, concat_axis=0, tiled=True)
    own = jnp.sum(cross, axis=0, keepdims=True)
    own = jnp.broadcast_to(own, (group, rows // LANES, LANES))
    cross = lax.all_to_all(own, chips, split_axis=0, concat_axis=0, tiled=True)
    cross = cross.reshape(group, rows)
    other = lax.ppermute(cross, "core", swap)
    upper = jnp.where(side == 0, cross, other)
    lower = jnp.where(side == 0, other, cross)
    cross = jnp.concatenate([upper, lower], axis=0)
    scale = 1.0 / (float(val_width * val_devices) ** 0.5 * blur)
    coupled = pl.pallas_call(
        functools.partial(sinkhorn_kernel, scale),
        out_shape=jax.ShapeDtypeStruct((rows, part), jnp.float32),
        in_specs=[pl.BlockSpec(memory_space=pltpu.VMEM)] * 2,
        out_specs=pl.BlockSpec(memory_space=pltpu.VMEM),
        compiler_params=pltpu.CompilerParams(vmem_limit_bytes=16 * 2**20),
    )(cross, noise_part)
    coupled = coupled.reshape(dp_devices, row_count, part)
    coupled = lax.all_to_all(coupled, dp, split_axis=0, concat_axis=0, tiled=True)
    target, mixed = mix(times, coupled, data, val_devices)
    moved = lax.all_to_all(mixed, val, split_axis=0, concat_axis=0, tiled=True)
    moved = moved.reshape(CH, row_count, strip)
    side = side.astype(jnp.int32).reshape(1)
    x, stats, w_small, scales = token_stats(moved, w_patch, patch_bias, norm_gain, order)
    x, w_own = lax.optimization_barrier((x, w_own))
    w_other = lax.ppermute(w_own, "core", [(0, 1), (1, 0)])
    qkv, normed = first_half(side, x, stats, w_small, scales, w_own, (256, 512, 768, 512, 256), 256)
    qkv = second_half(side, normed, w_other, qkv, (768, 768, 512, 256), 256)
    return (qkv.reshape(row_count, -1, 2 * half), target)


def solution(mesh):
    dp, val = ("y", "z"), ("x", "core")
    fine = Mesh(mesh.devices.reshape(4, 8, -1, 2), dp + val)
    return jax.shard_map(
        per_device,
        mesh=fine,
        in_specs=(P(dp, val), P(dp, val), P(dp), P(), P(), P(), P(dp, None)),
        out_specs=(P(dp, val, None), P(dp, val)),
        check_vma=False,
    )
```
